32 devices in a mesh: frame: 4 (over y, core), tok: 8 (over z, x).
Axes of the slice: x: 2, y: 2, z: 4, core: 2. Of those that a mesh axis runs over, the one named last changes fastest.
Arguments:
- inputs: bfloat16 [4, 6144, 512], P('frame', 'tok'), may hold values from -16 to 16
- kv_weight: bfloat16 [512, 2048], replicated, may hold values from -0.25 to 0.25
- latent_queries: bfloat16 [1024, 1024], P('tok'), may hold values from -21 to 21
- mix_gain: float32 [3072], replicated, may hold values from 0.5 to 2
- mix_weight: bfloat16 [3072, 1024], P(None, 'tok'), may hold values from -0.109375 to 0.109375
- output_queries: bfloat16 [4, 1024, 1024], P('frame', 'tok'), may hold values from -28 to 28
Outputs:
- decoded: float32 [4, 1024, 1024], P('frame', 'tok')
The draws below stay inside these ranges and needn't reach their ends.
All inputs are finite; a program needn't handle non-finite values.
Results may differ from the reference program's by a relative error of at most 0.035.
Values may be sent and summed in bfloat16 or wider, within the bound.
A program may use at most 128 MiB of HBM per device.

```python
import math
import jax
import jax.numpy as jnp
from jax import lax

C = 512
D = 1024
LATENTS = 1024
HEADS = 8
HEAD_DIM = 128
IN_DEV = 768
FRAMES = 4
INPUTS = 6144
OUTPUTS = 1024
N_TOK = 8


def draw_inputs(key, part):
    key_base, key_frame = jax.random.split(key)
    ramp = 3.0 ** (jnp.arange(FRAMES, dtype=jnp.float32) / max(FRAMES - 1, 1))
    jitter = jax.random.uniform(key_frame, (FRAMES,), jnp.float32, 0.8, 1.25)
    base_draw = jnp.clip(jax.random.normal(key_base, (FRAMES, INPUTS, C), jnp.float32), -4.0, 4.0)
    return (base_draw * (ramp * jitter)[:, None, None]).astype(jnp.bfloat16)


def spread_queries(key, count):
    key_base = jax.random.fold_in(jax.random.fold_in(key, 7), 0)
    base_draw = jnp.clip(jax.random.normal(key_base, (count, D), jnp.float32), -4.0, 4.0)
    return base_draw.astype(jnp.bfloat16)


def draw_latent_queries(key, part):
    return spread_queries(key, LATENTS)


def draw_output_queries(key, part):
    frame_keys = jax.random.split(jax.random.fold_in(key, 11), FRAMES)
    return jax.vmap(lambda frame_key: spread_queries(frame_key, OUTPUTS))(frame_keys)


def levels(rng, shape, shards, least, high):
    factor_of = 1.0
    for dim, blocks in shards:
        steps = jax.random.uniform(jax.random.fold_in(jax.random.fold_in(rng, 6), dim), (blocks,), jnp.float32, least / len(shards), high / len(shards))
        factor_of = factor_of * jnp.repeat(jnp.exp(steps), shape[dim] // blocks).reshape((-1,) + (1,) * (len(shape) - 1 - dim))
    return factor_of


def centred(key, shape, deviation, reach, cuts=(), kind=jnp.bfloat16):
    level = levels(key, shape, cuts, -0.22, 0.18) if cuts else 1.0
    result = jax.random.normal(key, shape, jnp.float32) * deviation * level
    return jnp.minimum(jnp.maximum(result, -reach), reach).astype(kind)


def setup_inputs(seed: int = 0) -> dict:
    arg_keys = jax.random.split(jax.random.key(seed), 7)
    inputs = draw_inputs(jax.random.fold_in(arg_keys[6], 71), 0)
    kv_weight = centred(arg_keys[1], (C, 2 * D), C ** -0.5, 0.25)
    latent_queries = draw_latent_queries(jax.random.fold_in(arg_keys[6], 71), 0)
    mix_gain = jnp.clip(jnp.exp(jax.random.uniform(arg_keys[3], (3 * D,), jnp.float32, math.log(0.5), math.log(2.0))), 0.5, 2.0)
    mix_weight = centred(arg_keys[4], (3 * D, D), (3 * D) ** -0.5, 0.109375, ((1, 8),))
    output_queries = draw_output_queries(jax.random.fold_in(arg_keys[6], 71), 0)
    return {"inputs": inputs, "kv_weight": kv_weight, "latent_queries": latent_queries, "mix_gain": mix_gain, "mix_weight": mix_weight, "output_queries": output_queries}


def attend_heads(queries, keys, values):
    maxima = []
    numers = []
    denoms = []
    for head_index in range(HEADS):
        low_col = head_index * HEAD_DIM
        high_col = low_col + HEAD_DIM
        scores = lax.dot_general(queries[:, low_col:high_col], keys[:, low_col:high_col], (((1,), (1,)), ((), ())), preferred_element_type=jnp.float32) / math.sqrt(HEAD_DIM)
        row_peak = lax.optimization_barrier(jnp.max(scores, axis=1))
        weights = jnp.exp(scores - row_peak[:, None])
        denoms.append(lax.optimization_barrier(jnp.sum(weights, axis=1)))
        numers.append(jnp.dot(weights.astype(jnp.bfloat16), values[:, low_col:high_col], preferred_element_type=jnp.float32))
        maxima.append(row_peak)
    return (jnp.stack(maxima, axis=1), jnp.concatenate(numers, axis=1), jnp.stack(denoms, axis=1))

def decode_heads(queries, latent_rows):
    pieces = []
    for head_index in range(HEADS):
        low_col = head_index * HEAD_DIM
        high_col = low_col + HEAD_DIM
        scores = lax.dot_general(queries[:, low_col:high_col], latent_rows[:, low_col:high_col], (((1,), (1,)), ((), ())), preferred_element_type=jnp.float32) / math.sqrt(HEAD_DIM)
        row_peak = lax.optimization_barrier(jnp.max(scores, axis=1))
        weights = jnp.exp(scores - row_peak[:, None])
        denom_sum = lax.optimization_barrier(jnp.sum(weights, axis=1))
        summed = jnp.dot(weights.astype(jnp.bfloat16), latent_rows[:, low_col:high_col], preferred_element_type=jnp.float32)
        pieces.append(summed / denom_sum[:, None])
    return jnp.concatenate(pieces, axis=1)

def reference(inputs, kv_weight, latent_queries, mix_gain, mix_weight, output_queries):

    def encode_frame(frame_inputs):
        key_values = jnp.dot(frame_inputs, kv_weight, preferred_element_type=jnp.float32).astype(jnp.bfloat16)
        blocks = key_values.reshape(N_TOK, IN_DEV, 2 * D)

        def one_block(state_carry, block_rows):
            return (state_carry, attend_heads(latent_queries, block_rows[:, :D], block_rows[:, D:]))
        unused, parts = lax.scan(one_block, jnp.zeros((), jnp.float32), blocks)
        maxima, numers, denoms = parts
        peak_all = lax.optimization_barrier(jnp.max(maxima, axis=0))
        rescale = jnp.exp(maxima - peak_all[None])
        numer_terms = (numers.reshape(N_TOK, LATENTS, HEADS, HEAD_DIM) * rescale[:, :, :, None]).astype(jnp.bfloat16)
        denom_terms = (denoms * rescale).astype(jnp.bfloat16)
        numer_terms, denom_terms = lax.optimization_barrier((numer_terms, denom_terms))
        numerator = lax.optimization_barrier(jnp.sum(numer_terms.astype(jnp.float32), axis=0))
        denominator = lax.optimization_barrier(jnp.sum(denom_terms.astype(jnp.float32), axis=0))
        return (numerator / denominator[:, :, None]).reshape(LATENTS, D).astype(jnp.bfloat16)
    latents = lax.map(encode_frame, inputs)
    prior_one = jnp.concatenate([jnp.zeros((1, LATENTS, D), jnp.bfloat16), latents[:-1]], axis=0)
    prior_two = jnp.concatenate([jnp.zeros((2, LATENTS, D), jnp.bfloat16), latents[:-2]], axis=0)[:FRAMES]
    joined = jnp.concatenate([latents, prior_one, prior_two], axis=2).astype(jnp.float32)
    inverse = lax.rsqrt(lax.optimization_barrier(jnp.mean(joined * joined, axis=2)) + 1e-06)
    scaled = (joined * mix_gain).astype(jnp.bfloat16)
    product = jnp.dot(scaled.reshape(FRAMES * LATENTS, 3 * D), mix_weight, preferred_element_type=jnp.float32).reshape(FRAMES, LATENTS, D)
    mixed = jax.nn.gelu(product * inverse[:, :, None], approximate=False).astype(jnp.bfloat16)

    def decode_frame(frame_pair):
        return decode_heads(frame_pair[0], frame_pair[1])
    return lax.map(decode_frame, (output_queries, mixed))
```

```python
import functools
import math

import jax
import jax.numpy as jnp
from jax import lax
from jax.experimental import pallas as pl
from jax.experimental.pallas import tpu as pltpu
from jax.sharding import PartitionSpec as P

HEADS = 8
HEAD_DIM = 128


def from_behind(block, axis, distance):
    devices = range(lax.axis_size(axis))
    route = [(i - distance, i) for i in devices if i - distance in devices]
    return lax.ppermute(block, axis, route)


def attend_heads(queries, keys, values, head_count, head_dim):
    maxima = []
    numers = []
    denoms = []
    for head_index in range(head_count):
        low_col = head_index * head_dim
        high_col = low_col + head_dim
        scores = lax.dot_general(
            queries[:, low_col:high_col],
            keys[:, low_col:high_col],
            (((1,), (1,)), ((), ())),
            preferred_element_type=jnp.float32,
        ) / math.sqrt(head_dim)
        row_peak = jnp.max(scores, axis=1)
        weights = jnp.exp(scores - row_peak[:, None])
        denoms.append(jnp.sum(weights, axis=1))
        numers.append(
            jnp.dot(
                weights.astype(jnp.bfloat16),
                values[:, low_col:high_col],
                preferred_element_type=jnp.float32,
            )
        )
        maxima.append(row_peak)
    return (jnp.stack(maxima, axis=1), jnp.concatenate(numers, axis=1), jnp.stack(denoms, axis=1))


def finish_latents(numerator, denominator, head_count, head_dim):
    row_count = numerator.shape[0]
    shaped = numerator.reshape(row_count, head_count, head_dim) / denominator[:, :, None]
    return shaped.reshape(row_count, head_count * head_dim).astype(jnp.bfloat16)


def project_cols(latent_part, gain_part, weight_part):
    scaled = (latent_part.astype(jnp.float32) * gain_part).astype(jnp.bfloat16)
    return lax.dot_general(
        weight_part, scaled, (((0,), (1,)), ((), ())), preferred_element_type=jnp.float32
    )


def local(inputs, kv_weight, latent_queries, mix_gain, mix_weight, output_queries):
    head_count = HEADS
    head_dim = HEAD_DIM
    latent_width = head_count * head_dim
    frame_inputs = inputs[0]
    queries = lax.all_gather(latent_queries, "tok", axis=0, tiled=True)
    key_values = jnp.dot(frame_inputs, kv_weight, preferred_element_type=jnp.float32).astype(
        jnp.bfloat16
    )
    maxima, numers, denoms = attend_heads(
        queries, key_values[:, :latent_width], key_values[:, latent_width:], head_count, head_dim
    )
    peak_all = lax.pmax(maxima.astype(jnp.bfloat16), "tok").astype(maxima.dtype)
    rescale = jnp.exp(maxima - peak_all)
    latent_count = queries.shape[0]
    numer_terms = (
        numers.reshape(latent_count, head_count, head_dim) * rescale[:, :, None]
    ).reshape(latent_count, latent_width)
    denom_terms = denoms * rescale
    numerator, denominator = (
        lax.psum(numer_terms.astype(jnp.bfloat16), "tok").astype(jnp.float32),
        lax.psum(denom_terms.astype(jnp.bfloat16), "tok").astype(jnp.float32),
    )
    latents = finish_latents(numerator, denominator, head_count, head_dim)
    latent_f32 = latents.astype(jnp.float32)
    own_squares = jnp.sum(latent_f32 * latent_f32, axis=1)
    term_now = project_cols(latents, mix_gain[:latent_width], mix_weight[:latent_width])
    term_one, squares_one = (
        from_behind(
            project_cols(
                latents,
                mix_gain[latent_width : 2 * latent_width],
                mix_weight[latent_width : 2 * latent_width],
            ).astype(jnp.bfloat16),
            "frame",
            1,
        ).astype(jnp.float32),
        from_behind(own_squares.astype(jnp.bfloat16), "frame", 1).astype(own_squares.dtype),
    )
    term_two, squares_two = (
        from_behind(
            project_cols(
                latents, mix_gain[2 * latent_width :], mix_weight[2 * latent_width :]
            ).astype(jnp.bfloat16),
            "frame",
            2,
        ).astype(jnp.float32),
        from_behind(own_squares.astype(jnp.bfloat16), "frame", 2).astype(own_squares.dtype),
    )
    summed = term_now + term_one + term_two
    squares = own_squares + squares_one + squares_two
    inverse = lax.rsqrt(squares / (3 * latent_width) + 1e-06)
    mixed_cols = jax.nn.gelu(summed * inverse[None, :], approximate=False).astype(jnp.bfloat16)
    mixed_t = lax.all_gather(mixed_cols, "tok", axis=0, tiled=True)
    frame_queries = output_queries[0]
    pieces = []
    for head_index in range(head_count):
        low_col = head_index * head_dim
        high_col = low_col + head_dim
        scores = jnp.dot(
            frame_queries[:, low_col:high_col],
            mixed_t[low_col:high_col],
            preferred_element_type=jnp.float32,
        ) / math.sqrt(head_dim)
        row_peak = jnp.max(scores, axis=1)
        weights = jnp.exp(scores - row_peak[:, None])
        denom_sum = jnp.sum(weights, axis=1)
        head_sum = lax.dot_general(
            weights.astype(jnp.bfloat16),
            mixed_t[low_col:high_col],
            (((1,), (1,)), ((), ())),
            preferred_element_type=jnp.float32,
        )
        pieces.append(head_sum / denom_sum[:, None])
    result = jnp.concatenate(pieces, axis=1)
    return result[None]


MESH = pl.DeviceIdType.MESH
LOG2E = 1.4426950408889634


def dot_nt(a, b):
    return lax.dot_general(a, b, (((1,), (1,)), ((), ())), preferred_element_type=jnp.float32)


def attend_columns(keys, values_t, queries, factor):
    scores = dot_nt(keys, queries)
    if factor is not None:
        scores = scores * factor
    peak = jnp.max(scores, axis=0, keepdims=True)
    weights = jnp.exp2(scores - peak)
    denom = jnp.sum(weights, axis=0, keepdims=True)
    numer = jnp.dot(values_t, weights.astype(jnp.bfloat16), preferred_element_type=jnp.float32)
    return numer, peak, denom


def copy_ids(n_tok, pairs):
    names = []
    for j in range(1, pairs):
        names += [("qz", j), ("qx", j), ("nz", j), ("sz", j), ("lz", j), ("lx", j)]
    for j in range(pairs):
        names += [("nx", j), ("sx", j), ("t1", j), ("t2", j)]
    for k in range(1, n_tok):
        names += [("qc", k), ("oq", k), ("out", k)]
    names += [("qx", 0), ("lx", 0)]
    return {name: i for i, name in enumerate(names)}


def window_kernel(
    n_tok, n_frame, x_ref, kvw_ref, lq_ref, gain_ref, w_ref, oq_ref, out_ref,
    qbuf, kbuf, vbuf, w3, own_n, own_s, xs_n, xs_s, xr_n, xr_s, zs_n, zs_s, zr_n, zr_s,
    lat, now, sq_own, ts1, ts2, tr1, tr2, mix_t, mix, oqbuf, osend, obuf, send_sem, recv_sem,
):
    heads = n_tok
    pairs = n_tok // 2
    rows = lq_ref.shape[0]
    dim = w_ref.shape[1]
    width = heads * dim
    qrows = oq_ref.shape[1]
    factor = LOG2E / math.sqrt(dim)
    ids = copy_ids(n_tok, pairs)
    fi = lax.axis_index("frame")
    ti = lax.axis_index("tok")
    half = rows // 2
    mine = lax.rem(fi, 2)
    sibling = fi + 1 - 2 * mine
    started = []

    def flip(k):
        out = 0
        bit = 1
        while bit < n_tok:
            b = lax.rem(lax.div(ti, bit), 2)
            out = out + bit * ((1 - b) if (k & bit) else b)
            bit *= 2
        return out

    peer = [flip(k) for k in range(n_tok)]

    def copy(name, src, dst, where):
        i = ids[name]
        return pltpu.make_async_remote_copy(
            src_ref=src, dst_ref=dst, send_sem=send_sem.at[i], recv_sem=recv_sem.at[i],
            device_id=where, device_id_type=MESH,
        )

    def send(name, src, dst, where):
        c = copy(name, src, dst, where)
        c.start()
        started.append(c)

    def arrived(name, dst, where):
        copy(name, dst, dst, where).wait_recv()

    def tok(k):
        return (fi, peer[k])

    barrier = pltpu.get_barrier_semaphore()
    for k in range(1, n_tok):
        pl.semaphore_signal(barrier, inc=1, device_id=tok(k), device_id_type=MESH)
    for o in range(1, n_frame):
        pl.semaphore_signal(
            barrier, inc=1, device_id=(lax.rem(fi + o, n_frame), ti), device_id_type=MESH
        )
    pl.semaphore_wait(barrier, n_tok - 1 + n_frame - 1)

    here = pl.multiple_of(mine * half, half)
    there = pl.multiple_of((1 - mine) * half, half)

    def qpart(k, off):
        return qbuf.at[pl.ds(k * rows + off, half), :]

    own_half = lq_ref.at[pl.ds(here, half), :]
    for j in range(pairs - 1, 0, -1):
        send(("qz", j), own_half, qpart(2 * j, here), tok(2 * j))
    send(("qx", 0), own_half, qpart(1, here), tok(1))
    for k in range(n_tok - 1, 0, -1):
        cols = pl.ds(pl.multiple_of(peer[k] * dim, dim), dim)
        send(("oq", k), oq_ref.at[0, :, cols], oqbuf.at[pl.ds(k * qrows, qrows), :], tok(k))
    qbuf[0:rows, :] = lq_ref[...]
    own_cols = pl.ds(pl.multiple_of(ti * dim, dim), dim)
    oqbuf[0:qrows, :] = oq_ref[0, :, own_cols]

    def project_keys(i, carry):
        cols = pl.ds(pl.multiple_of(i * 2 * dim, 2 * dim), 2 * dim)
        k = jnp.dot(x_ref[0], kvw_ref[:, cols], preferred_element_type=jnp.float32)
        k = (k * factor).astype(jnp.bfloat16)
        kbuf[2 * i] = k[:, :dim]
        kbuf[2 * i + 1] = k[:, dim:]
        return carry

    lax.fori_loop(0, heads // 2, project_keys, 0)

    arrived(("qx", 0), qpart(1, here), tok(1))
    send(("qc", 1), qpart(1, here), qpart(1, here), (sibling, ti))
    for j in range(pairs - 1, 0, -1):
        arrived(("qz", j), qpart(2 * j, here), tok(2 * j))
        send(("qx", j), qpart(2 * j, here), qpart(2 * j + 1, here), tok(1))
        send(("qc", 2 * j), qpart(2 * j, here), qpart(2 * j, here), (sibling, ti))

    def project_values(i, carry):
        cols = pl.ds(pl.multiple_of(width + i * 2 * dim, 2 * dim), 2 * dim)
        v = jnp.dot(x_ref[0], kvw_ref[:, cols], preferred_element_type=jnp.float32)
        v = v.astype(jnp.bfloat16).T
        vbuf[2 * i] = v[:dim]
        vbuf[2 * i + 1] = v[dim:]
        return carry

    lax.fori_loop(0, heads // 2, project_values, 0)

    for j in range(pairs - 1, 0, -1):
        k = 2 * j + 1
        arrived(("qx", j), qpart(k, here), tok(1))
        send(("qc", k), qpart(k, here), qpart(k, here), (sibling, ti))

    for t in range(3):
        w_t = w_ref[t * width : (t + 1) * width, :].T.astype(jnp.float32)
        w3[t * dim : (t + 1) * dim, :] = (w_t * gain_ref[t : t + 1, :]).astype(jnp.bfloat16)

    def merge_x(j):
        arrived(("nx", j), xr_n.at[j], tok(1))
        arrived(("sx", j), xr_s.at[j], tok(1))
        m1, l1 = own_s[j, 0:heads, :], own_s[j, heads : 2 * heads, :]
        m2, l2 = xr_s[j, 0:heads, :], xr_s[j, heads : 2 * heads, :]
        m = jnp.maximum(m1, m2)
        a1, a2 = jnp.exp2(m1 - m), jnp.exp2(m2 - m)
        l = l1 * a1 + l2 * a2
        if j == 0:
            own_s[0, 0:heads, :] = m
            own_s[0, heads : 2 * heads, :] = l
        else:
            zs_s[j, 0:heads, :] = m
            zs_s[j, heads : 2 * heads, :] = l
        for h in range(heads):
            n = own_n[j, h] * a1[h : h + 1] + xr_n[j, h].astype(jnp.float32) * a2[h : h + 1]
            if j == 0:
                own_n[0, h] = n
            else:
                zs_n[j, h] = n.astype(jnp.bfloat16)
        if j > 0:
            send(("nz", j), zs_n.at[j], zr_n.at[j], tok(2 * j))
            send(("sz", j), zs_s.at[j], zr_s.at[j], tok(2 * j))

    for j in range(pairs - 1, -1, -1):
        for k in (2 * j, 2 * j + 1):
            if k > 0:
                arrived(("qc", k), qpart(k, there), (sibling, ti))

        def head_pair(i, carry, j=j):
            for u in range(2):
                h = 2 * i + u
                cols = pl.ds(pl.multiple_of(h * dim, dim), dim)
                q = qbuf[2 * j * rows : (2 * j + 2) * rows, cols]
                n, m, l = attend_columns(kbuf[h], vbuf[h], q, None)
                own_n[j, h] = n[:, :rows]
                own_s[j, pl.ds(h, 1), :] = m[:, :rows]
                own_s[j, pl.ds(heads + h, 1), :] = l[:, :rows]
                xs_n[j, h] = n[:, rows:].astype(jnp.bfloat16)
                xs_s[j, pl.ds(h, 1), :] = m[:, rows:]
                xs_s[j, pl.ds(heads + h, 1), :] = l[:, rows:]
            return carry

        lax.fori_loop(0, heads // 2, head_pair, 0)
        send(("nx", j), xs_n.at[j], xr_n.at[j], tok(1))
        send(("sx", j), xs_s.at[j], xr_s.at[j], tok(1))
        if j < pairs - 1:
            merge_x(j + 1)
    merge_x(0)

    for j in range(pairs - 1, 0, -1):
        arrived(("nz", j), zr_n.at[j], tok(2 * j))
        arrived(("sz", j), zr_s.at[j], tok(2 * j))
    peaks = [own_s[0, 0:heads, :]] + [zr_s[j, 0:heads, :] for j in range(1, pairs)]
    dens = [own_s[0, heads : 2 * heads, :]]
    dens += [zr_s[j, heads : 2 * heads, :] for j in range(1, pairs)]
    top = functools.reduce(jnp.maximum, peaks)
    scale = [jnp.exp2(p - top) for p in peaks]
    total = sum(d * s for d, s in zip(dens, scale))
    scale = [s / total for s in scale]
    for h in range(heads):
        n = own_n[0, h] * scale[0][h : h + 1]
        for j in range(1, pairs):
            n = n + zr_n[j, h].astype(jnp.float32) * scale[j][h : h + 1]
        lat[0, h * dim : (h + 1) * dim, :] = n.astype(jnp.bfloat16)

    for j in range(pairs - 1, 0, -1):
        send(("lz", j), lat.at[0], lat.at[2 * j], tok(2 * j))
    send(("lx", 0), lat.at[0], lat.at[1], tok(1))

    def mix_pair(c):
        both = jnp.concatenate([lat[2 * c], lat[2 * c + 1]], axis=1)
        wide = both.astype(jnp.float32)
        squares = jnp.sum(wide * wide, axis=0, keepdims=True)
        terms = jnp.dot(w3[...], both, preferred_element_type=jnp.float32)
        now[c] = terms[:dim]
        sq_own[c] = jnp.broadcast_to(squares, sq_own.shape[1:])
        sq = jnp.broadcast_to(squares, (16, 2 * rows)).astype(jnp.bfloat16)
        ts1[c, 0:dim, :] = terms[dim : 2 * dim].astype(jnp.bfloat16)
        ts1[c, dim : dim + 16, :] = sq
        ts2[c, 0:dim, :] = terms[2 * dim :].astype(jnp.bfloat16)
        ts2[c, dim : dim + 16, :] = sq

        @pl.when(fi < n_frame - 1)
        def _():
            copy(("t1", c), ts1.at[c], tr1.at[c], (lax.rem(fi + 1, n_frame), ti)).start()

        @pl.when(fi < n_frame - 2)
        def _():
            copy(("t2", c), ts2.at[c], tr2.at[c], (lax.rem(fi + 2, n_frame), ti)).start()

    order = [1, 2, 3] if pairs == 4 else list(range(1, pairs))
    for j in order:
        arrived(("lz", j), lat.at[2 * j], tok(2 * j))
        send(("lx", j), lat.at[2 * j], lat.at[2 * j + 1], tok(1))
    for c in [0] + order:
        arrived(("lx", c), lat.at[2 * c + 1], tok(1))
        mix_pair(c)

    @pl.when(fi < 1)
    def _():
        tr1[...] = jnp.zeros_like(tr1)

    @pl.when(fi < 2)
    def _():
        tr2[...] = jnp.zeros_like(tr2)

    for c in [0] + order:

        @pl.when(fi >= 1)
        def _():
            copy(("t1", c), ts1.at[c], tr1.at[c], (lax.rem(fi + 1, n_frame), ti)).wait_recv()

        @pl.when(fi >= 2)
        def _():
            copy(("t2", c), ts2.at[c], tr2.at[c], (lax.rem(fi + 2, n_frame), ti)).wait_recv()

        summed = now[c] + tr1[c, 0:dim, :].astype(jnp.float32) + tr2[c, 0:dim, :].astype(jnp.float32)
        squares = (
            sq_own[c, 0:1, :]
            + tr1[c, dim : dim + 16, :].astype(jnp.float32)[0:1]
            + tr2[c, dim : dim + 16, :].astype(jnp.float32)[0:1]
        )
        z = summed * lax.rsqrt(squares / (3 * width) + 1e-06)
        mixed = (0.5 * z * (1.0 + lax.erf(z * math.sqrt(0.5)))).astype(jnp.bfloat16)
        mix_t[:, c * 2 * rows : (c + 1) * 2 * rows] = mixed
        mix[c * 2 * rows : (c + 1) * 2 * rows, :] = mixed.T

    for k in range(1, n_tok):
        arrived(("oq", k), oqbuf.at[pl.ds(k * qrows, qrows), :], tok(k))
    for c in range(pairs - 1, -1, -1):
        q = oqbuf[2 * c * qrows : (2 * c + 2) * qrows, :]
        n, m, l = attend_columns(mix[...], mix_t[...], q, factor)
        o = (n / l).T
        for k in (2 * c, 2 * c + 1):
            part = o[(k - 2 * c) * qrows : (k - 2 * c + 1) * qrows]
            if k == 0:
                out_ref[0, :, own_cols] = part
            else:
                osend[k] = part.astype(jnp.bfloat16)
                send(("out", k), osend.at[k], obuf.at[k], tok(k))
    for k in range(n_tok - 1, 0, -1):
        arrived(("out", k), obuf.at[k], tok(k))
        cols = pl.ds(pl.multiple_of(peer[k] * dim, dim), dim)
        out_ref[0, :, cols] = obuf[k].astype(jnp.float32)

    for c in started:
        c.wait_send()
    for c in range(pairs):

        @pl.when(fi < n_frame - 1)
        def _():
            copy(("t1", c), ts1.at[c], tr1.at[c], (lax.rem(fi + 1, n_frame), ti)).wait_send()

        @pl.when(fi < n_frame - 2)
        def _():
            copy(("t2", c), ts2.at[c], tr2.at[c], (lax.rem(fi + 2, n_frame), ti)).wait_send()


def local_fused(inputs, kv_weight, latent_queries, mix_gain, mix_weight, output_queries):
    n_tok = lax.axis_size("tok")
    n_frame = lax.axis_size("frame")
    pairs = n_tok // 2
    heads = HEADS
    dim = HEAD_DIM
    width = heads * dim
    n_in = inputs.shape[1]
    rows = latent_queries.shape[0]
    qrows = output_queries.shape[1]
    bf16, f32 = jnp.bfloat16, jnp.float32
    stats = (pairs, 2 * heads, rows)
    block = (pairs, heads, dim, rows)
    n_ids = len(copy_ids(n_tok, pairs))
    vmem = pltpu.VMEM
    scratch = [
        vmem((n_tok * rows, width), bf16),
        vmem((heads, n_in, dim), bf16),
        vmem((heads, dim, n_in), bf16),
        vmem((3 * dim, width), bf16),
        vmem(block, f32), vmem(stats, f32),
        vmem(block, bf16), vmem(stats, f32),
        vmem(block, bf16), vmem(stats, f32),
        vmem(block, bf16), vmem(stats, f32),
        vmem(block, bf16), vmem(stats, f32),
        vmem((n_tok, width, rows), bf16),
        vmem((pairs, dim, 2 * rows), f32),
        vmem((pairs, 8, 2 * rows), f32),
        vmem((pairs, dim + 16, 2 * rows), bf16),
        vmem((pairs, dim + 16, 2 * rows), bf16),
        vmem((pairs, dim + 16, 2 * rows), bf16),
        vmem((pairs, dim + 16, 2 * rows), bf16),
        vmem((dim, n_tok * rows), bf16),
        vmem((n_tok * rows, dim), bf16),
        vmem((n_tok * qrows, dim), bf16),
        vmem((n_tok, qrows, dim), bf16),
        vmem((n_tok, qrows, dim), bf16),
        pltpu.SemaphoreType.DMA((n_ids,)),
        pltpu.SemaphoreType.DMA((n_ids,)),
    ]
    return pl.pallas_call(
        functools.partial(window_kernel, n_tok, n_frame),
        out_shape=jax.ShapeDtypeStruct((1, qrows, width), f32),
        in_specs=[pl.BlockSpec(memory_space=pltpu.VMEM)] * 6,
        out_specs=pl.BlockSpec(memory_space=pltpu.VMEM),
        scratch_shapes=scratch,
        compiler_params=pltpu.CompilerParams(
            collective_id=0, has_side_effects=True, vmem_limit_bytes=56 * 1024 * 1024
        ),
    )(inputs, kv_weight, latent_queries, mix_gain.reshape(3, width), mix_weight, output_queries)


def pick_local(mesh):
    n_tok, n_frame = mesh.shape["tok"], mesh.shape["frame"]
    fits = n_tok == HEADS and n_frame % 2 == 0 and n_frame > 2
    return local_fused if fits else local


def solution(mesh):
    return jax.shard_map(
        pick_local(mesh),
        mesh=mesh,
        in_specs=(
            P("frame", "tok", None),
            P(),
            P("tok", None),
            P(),
            P(None, "tok"),
            P("frame", "tok", None),
        ),
        out_specs=P("frame", "tok", None),
        check_vma=False,
    )
```

```python
import functools
import math

import jax
import jax.numpy as jnp
from jax import lax
from jax.experimental import pallas as pl
from jax.experimental.pallas import tpu as pltpu
from jax.sharding import PartitionSpec as P

HEADS = 8
HEAD_DIM = 128


def from_behind(block, axis, distance):
    devices = range(lax.axis_size(axis))
    route = [(i - distance, i) for i in devices if i - distance in devices]
    return lax.ppermute(block, axis, route)


def attend_heads(queries, keys, values, head_count, head_dim):
    maxima = []
    numers = []
    denoms = []
    for head_index in range(head_count):
        low_col = head_index * head_dim
        high_col = low_col + head_dim
        scores = lax.dot_general(
            queries[:, low_col:high_col],
            keys[:, low_col:high_col],
            (((1,), (1,)), ((), ())),
            preferred_element_type=jnp.float32,
        ) / math.sqrt(head_dim)
        row_peak = jnp.max(scores, axis=1)
        weights = jnp.exp(scores - row_peak[:, None])
        denoms.append(jnp.sum(weights, axis=1))
        numers.append(
            jnp.dot(
                weights.astype(jnp.bfloat16),
                values[:, low_col:high_col],
                preferred_element_type=jnp.float32,
            )
        )
        maxima.append(row_peak)
    return (jnp.stack(maxima, axis=1), jnp.concatenate(numers, axis=1), jnp.stack(denoms, axis=1))


def finish_latents(numerator, denominator, head_count, head_dim):
    row_count = numerator.shape[0]
    shaped = numerator.reshape(row_count, head_count, head_dim) / denominator[:, :, None]
    return shaped.reshape(row_count, head_count * head_dim).astype(jnp.bfloat16)


def project_cols(latent_part, gain_part, weight_part):
    scaled = (latent_part.astype(jnp.float32) * gain_part).astype(jnp.bfloat16)
    return lax.dot_general(
        weight_part, scaled, (((0,), (1,)), ((), ())), preferred_element_type=jnp.float32
    )


def local(inputs, kv_weight, latent_queries, mix_gain, mix_weight, output_queries):
    head_count = HEADS
    head_dim = HEAD_DIM
    latent_width = head_count * head_dim
    frame_inputs = inputs[0]
    queries = lax.all_gather(latent_queries, "tok", axis=0, tiled=True)
    key_values = jnp.dot(frame_inputs, kv_weight, preferred_element_type=jnp.float32).astype(
        jnp.bfloat16
    )
    maxima, numers, denoms = attend_heads(
        queries, key_values[:, :latent_width], key_values[:, latent_width:], head_count, head_dim
    )
    peak_all = lax.pmax(maxima.astype(jnp.bfloat16), "tok").astype(maxima.dtype)
    rescale = jnp.exp(maxima - peak_all)
    latent_count = queries.shape[0]
    numer_terms = (
        numers.reshape(latent_count, head_count, head_dim) * rescale[:, :, None]
    ).reshape(latent_count, latent_width)
    denom_terms = denoms * rescale
    numerator, denominator = (
        lax.psum(numer_terms.astype(jnp.bfloat16), "tok").astype(jnp.float32),
        lax.psum(denom_terms.astype(jnp.bfloat16), "tok").astype(jnp.float32),
    )
    latents = finish_latents(numerator, denominator, head_count, head_dim)
    latent_f32 = latents.astype(jnp.float32)
    own_squares = jnp.sum(latent_f32 * latent_f32, axis=1)
    term_now = project_cols(latents, mix_gain[:latent_width], mix_weight[:latent_width])
    term_one, squares_one = (
        from_behind(
            project_cols(
                latents,
                mix_gain[latent_width : 2 * latent_width],
                mix_weight[latent_width : 2 * latent_width],
            ).astype(jnp.bfloat16),
            "frame",
            1,
        ).astype(jnp.float32),
        from_behind(own_squares.astype(jnp.bfloat16), "frame", 1).astype(own_squares.dtype),
    )
    term_two, squares_two = (
        from_behind(
            project_cols(
                latents, mix_gain[2 * latent_width :], mix_weight[2 * latent_width :]
            ).astype(jnp.bfloat16),
            "frame",
            2,
        ).astype(jnp.float32),
        from_behind(own_squares.astype(jnp.bfloat16), "frame", 2).astype(own_squares.dtype),
    )
    summed = term_now + term_one + term_two
    squares = own_squares + squares_one + squares_two
    inverse = lax.rsqrt(squares / (3 * latent_width) + 1e-06)
    mixed_cols = jax.nn.gelu(summed * inverse[None, :], approximate=False).astype(jnp.bfloat16)
    mixed_t = lax.all_gather(mixed_cols, "tok", axis=0, tiled=True)
    frame_queries = output_queries[0]
    pieces = []
    for head_index in range(head_count):
        low_col = head_index * head_dim
        high_col = low_col + head_dim
        scores = jnp.dot(
            frame_queries[:, low_col:high_col],
            mixed_t[low_col:high_col],
            preferred_element_type=jnp.float32,
        ) / math.sqrt(head_dim)
        row_peak = jnp.max(scores, axis=1)
        weights = jnp.exp(scores - row_peak[:, None])
        denom_sum = jnp.sum(weights, axis=1)
        head_sum = lax.dot_general(
            weights.astype(jnp.bfloat16),
            mixed_t[low_col:high_col],
            (((1,), (1,)), ((), ())),
            preferred_element_type=jnp.float32,
        )
        pieces.append(head_sum / denom_sum[:, None])
    result = jnp.concatenate(pieces, axis=1)
    return result[None]


MESH = pl.DeviceIdType.MESH
LOG2E = 1.4426950408889634


def dot_nt(a, b):
    return lax.dot_general(a, b, (((1,), (1,)), ((), ())), preferred_element_type=jnp.float32)


def attend_columns(keys, values_t, queries, factor):
    scores = dot_nt(keys, queries)
    if factor is not None:
        scores = scores * factor
    peak = jnp.max(scores, axis=0, keepdims=True)
    weights = jnp.exp2(scores - peak)
    denom = jnp.sum(weights, axis=0, keepdims=True)
    numer = jnp.dot(values_t, weights.astype(jnp.bfloat16), preferred_element_type=jnp.float32)
    return numer, peak, denom


def copy_ids(n_tok, pairs):
    names = []
    for j in range(1, pairs):
        names += [("qz", j), ("qx", j)]
    for j in range(pairs):
        names += [("t1", j), ("t2", j), ("mx", j)]
        for g in range(2):
            names += [(n, j, g) for n in ("nx", "sx", "nz", "sz", "lz", "fz")]
    for k in range(1, n_tok):
        names += [("qc", k), ("oq", k), ("out", k)]
    names += [("qx", 0), ("wx",), ("wc",)]
    return {name: i for i, name in enumerate(names)}


def window_kernel(
    n_tok, n_frame, x_ref, kvw_ref, lq_ref, gain_ref, w_ref, oq_ref, out_ref,
    qbuf, kbuf, vbuf, wbuf, w3, own_n, own_s, xs_n, xs_s, xr_n, xr_s, zs_n, zs_s, zr_n, zr_s,
    lat, now, sq_own, ts1, ts2, tr1, tr2, msend, mixbuf, mix_t, mix, oqbuf, osend, obuf, send_sem, recv_sem,
):
    heads = n_tok
    pairs = n_tok // 2
    rows = lq_ref.shape[0]
    dim = w_ref.shape[1]
    width = heads * dim
    qrows = oq_ref.shape[1]
    factor = LOG2E / math.sqrt(dim)
    ids = copy_ids(n_tok, pairs)
    fi = lax.axis_index("frame")
    ti = lax.axis_index("tok")
    half = rows // 2
    mine = lax.rem(fi, 2)
    sibling = fi + 1 - 2 * mine
    started = []

    def flip(k):
        out = 0
        bit = 1
        while bit < n_tok:
            b = lax.rem(lax.div(ti, bit), 2)
            out = out + bit * ((1 - b) if (k & bit) else b)
            bit *= 2
        return out

    peer = [flip(k) for k in range(n_tok)]

    def copy(name, src, dst, where, send_name=None):
        return pltpu.make_async_remote_copy(
            src_ref=src, dst_ref=dst,
            send_sem=send_sem.at[ids[send_name or name]], recv_sem=recv_sem.at[ids[name]],
            device_id=where, device_id_type=MESH,
        )

    def send(name, src, dst, where):
        c = copy(name, src, dst, where)
        c.start()
        started.append(c)

    def arrived(name, dst, where):
        copy(name, dst, dst, where).wait_recv()

    def tok(k):
        return (fi, peer[k])

    barrier = pltpu.get_barrier_semaphore()
    for k in range(1, n_tok):
        pl.semaphore_signal(barrier, inc=1, device_id=tok(k), device_id_type=MESH)
    for o in range(1, n_frame):
        pl.semaphore_signal(
            barrier, inc=1, device_id=(lax.rem(fi + o, n_frame), ti), device_id_type=MESH
        )
    pl.semaphore_wait(barrier, n_tok - 1 + n_frame - 1)

    here = pl.multiple_of(mine * half, half)
    there = pl.multiple_of((1 - mine) * half, half)

    def qpart(k, off):
        return qbuf.at[pl.ds(k * rows + off, half), :]

    own_half = lq_ref.at[pl.ds(here, half), :]
    for j in range(pairs - 1, 0, -1):
        send(("qz", j), own_half, qpart(2 * j, here), tok(2 * j))
    send(("qx", 0), own_half, qpart(1, here), tok(1))
    qbuf[0:rows, :] = lq_ref[...]
    own_cols = pl.ds(pl.multiple_of(ti * dim, dim), dim)
    oqbuf[0:qrows, :] = oq_ref[0, :, own_cols]

    def project_keys(i, carry):
        cols = pl.ds(pl.multiple_of(i * 2 * dim, 2 * dim), 2 * dim)
        k = jnp.dot(x_ref[0], kvw_ref[:, cols], preferred_element_type=jnp.float32)
        k = k.astype(jnp.bfloat16)
        kbuf[2 * i] = k[:, :dim]
        kbuf[2 * i + 1] = k[:, dim:]
        return carry

    lax.fori_loop(0, heads // 2, project_keys, 0)

    arrived(("qx", 0), qpart(1, here), tok(1))
    send(("qc", 1), qpart(1, here), qpart(1, here), (sibling, ti))
    def project_values(i, carry):
        cols = pl.ds(pl.multiple_of(width + i * 2 * dim, 2 * dim), 2 * dim)
        v = jnp.dot(x_ref[0], kvw_ref[:, cols], preferred_element_type=jnp.float32)
        v = v.astype(jnp.bfloat16).T
        vbuf[2 * i] = v[:dim]
        vbuf[2 * i + 1] = v[dim:]
        return carry

    lax.fori_loop(0, heads // 2, project_values, 0)

    group = heads // 2

    def heads_of(g):
        return pl.ds(g * group, group)

    def merge_x(j, g):
        arrived(("nx", j, g), xr_n.at[j, heads_of(g)], tok(1))
        arrived(("sx", j, g), xr_s.at[j, g], tok(1))
        m1, l1 = own_s[j, g, 0:group, :], own_s[j, g, group:, :]
        m2, l2 = xr_s[j, g, 0:group, :], xr_s[j, g, group:, :]
        m = jnp.maximum(m1, m2)
        a1, a2 = jnp.exp2(m1 - m), jnp.exp2(m2 - m)
        target = own_s if j == 0 else zs_s
        target[j, g, 0:group, :] = m
        target[j, g, group:, :] = l1 * a1 + l2 * a2
        for i in range(group):
            h = g * group + i
            n = own_n[j, h] * a1[i : i + 1] + xr_n[j, h].astype(jnp.float32) * a2[i : i + 1]
            if j == 0:
                own_n[0, h] = n
            else:
                zs_n[j, h] = n.astype(jnp.bfloat16)
        if j > 0:
            where = tok(2 * j)
            send(("nz", j, g), zs_n.at[j, heads_of(g)], zr_n.at[j, heads_of(g)], where)
            send(("sz", j, g), zs_s.at[j, g], zr_s.at[j, g], where)

    def attend_unit(j, g):
        def head_pair(i, carry):
            for u in range(2):
                r = 2 * i + u
                h = g * group + r
                cols = pl.ds(pl.multiple_of(h * dim, dim), dim)
                q = qbuf[2 * j * rows : (2 * j + 2) * rows, cols]
                n, m, l = attend_columns(kbuf[h], vbuf[h], q, factor)
                own_n[j, h] = n[:, :rows]
                own_s[j, g, pl.ds(r, 1), :] = m[:, :rows]
                own_s[j, g, pl.ds(group + r, 1), :] = l[:, :rows]
                xs_n[j, h] = n[:, rows:].astype(jnp.bfloat16)
                xs_s[j, g, pl.ds(r, 1), :] = m[:, rows:]
                xs_s[j, g, pl.ds(group + r, 1), :] = l[:, rows:]
            return carry

        lax.fori_loop(0, group // 2, head_pair, 0)
        send(("nx", j, g), xs_n.at[j, heads_of(g)], xr_n.at[j, heads_of(g)], tok(1))
        send(("sx", j, g), xs_s.at[j, g], xr_s.at[j, g], tok(1))

    def wait_queries(j):
        for k in (2 * j, 2 * j + 1):
            if k > 0:
                arrived(("qc", k), qpart(k, there), (sibling, ti))

    wait_queries(0)
    attend_unit(0, 0)
    for j in range(pairs - 1, 0, -1):
        arrived(("qz", j), qpart(2 * j, here), tok(2 * j))
        send(("qx", j), qpart(2 * j, here), qpart(2 * j + 1, here), tok(1))
        send(("qc", 2 * j), qpart(2 * j, here), qpart(2 * j, here), (sibling, ti))
    attend_unit(0, 1)
    merge_x(0, 0)
    for j in range(pairs - 1, 0, -1):
        k = 2 * j + 1
        arrived(("qx", j), qpart(k, here), tok(1))
        send(("qc", k), qpart(k, here), qpart(k, here), (sibling, ti))
    for k in range(n_tok - 1, 0, -1):
        cols = pl.ds(pl.multiple_of(peer[k] * dim, dim), dim)
        send(("oq", k), oq_ref.at[0, :, cols], oqbuf.at[pl.ds(k * qrows, qrows), :], tok(k))
    before = (0, 1)
    for j in range(pairs - 1, 0, -1):
        wait_queries(j)
        for g in range(2):
            attend_unit(j, g)
            merge_x(*before)
            before = (j, g)
    w_rows = w_ref.shape[0] // 2
    w_here = pl.ds(pl.multiple_of(mine * w_rows, w_rows), w_rows)
    w_there = pl.ds(pl.multiple_of((1 - mine) * w_rows, w_rows), w_rows)
    send(("wx",), w_ref.at[w_here, :], wbuf.at[w_here, :], tok(1))
    merge_x(*before)

    line = lax.div(ti, 2)
    middle = jnp.logical_and(line > 0, line < pairs - 1)

    def lat_part(slot, g):
        return lat.at[slot, pl.ds(g * group * dim, group * dim), :]

    def forward(slot, g):
        far, near = tok(2 * (pairs - 1)), tok(2)
        plan = {0: (3, far), 1: (2, far), 3: (2, near), 2: (3, near)}
        there_slot, where = plan[slot]
        return copy(
            ("lz", there_slot, g), lat_part(slot, g), lat_part(there_slot, g), where, ("fz", slot, g)
        )

    def pass_on(slot):
        for g in range(2):
            arrived(("lz", slot, g), lat_part(slot, g), tok(2))
            forward(slot, g).start()

    for g in range(2):
        for j in range(pairs - 1, 0, -1):
            arrived(("nz", j, g), zr_n.at[j, heads_of(g)], tok(2 * j))
            arrived(("sz", j, g), zr_s.at[j, g], tok(2 * j))
        peaks = [own_s[0, g, 0:group, :]] + [zr_s[j, g, 0:group, :] for j in range(1, pairs)]
        dens = [own_s[0, g, group:, :]] + [zr_s[j, g, group:, :] for j in range(1, pairs)]
        top = functools.reduce(jnp.maximum, peaks)
        scale = [jnp.exp2(p - top) for p in peaks]
        total = sum(d * s for d, s in zip(dens, scale))
        scale = [s / total for s in scale]
        for i in range(group):
            h = g * group + i
            n = own_n[0, h] * scale[0][i : i + 1]
            for j in range(1, pairs):
                n = n + zr_n[j, h].astype(jnp.float32) * scale[j][i : i + 1]
            lat[0, h * dim : (h + 1) * dim, :] = n.astype(jnp.bfloat16)
        send(("lz", 1, g), lat_part(0, g), lat_part(1, g), tok(2))

        @pl.when(middle)
        def _():
            forward(0, g).start()

    def mix_weights(source, place):
        for t in range(3):
            w_t = source[t * width : (t + 1) * width, :].T.astype(jnp.float32)
            gain = gain_ref[t * width : (t + 1) * width].reshape(1, width)
            at = 2 * t + place
            w3[at * dim : (at + 1) * dim, :] = (w_t * gain).astype(jnp.bfloat16)

    arrived(("wx",), wbuf.at[w_here, :], tok(1))
    send(("wc",), wbuf.at[w_here, :], wbuf.at[w_here, :], (sibling, ti))
    mix_weights(w_ref, 0)

    @pl.when(middle)
    def _():
        pass_on(1)

    arrived(("wc",), wbuf.at[w_there, :], (sibling, ti))
    mix_weights(wbuf, 1)

    def mix_rows(c):
        block = lat[c]
        wide = block.astype(jnp.float32)
        squares = jnp.sum(wide * wide, axis=0, keepdims=True)
        terms = jnp.dot(w3[...], block, preferred_element_type=jnp.float32)
        now[c] = terms[: 2 * dim]
        sq_own[c] = jnp.broadcast_to(squares, sq_own.shape[1:])
        sq = jnp.broadcast_to(squares, (16, rows)).astype(jnp.bfloat16)
        ts1[c, 0 : 2 * dim, :] = terms[2 * dim : 4 * dim].astype(jnp.bfloat16)
        ts1[c, 2 * dim :, :] = sq
        ts2[c, 0 : 2 * dim, :] = terms[4 * dim :].astype(jnp.bfloat16)
        ts2[c, 2 * dim :, :] = sq

        @pl.when(fi < n_frame - 1)
        def _():
            copy(("t1", c), ts1.at[c], tr1.at[c], (lax.rem(fi + 1, n_frame), ti)).start()

        @pl.when(fi < n_frame - 2)
        def _():
            copy(("t2", c), ts2.at[c], tr2.at[c], (lax.rem(fi + 2, n_frame), ti)).start()

    @pl.when(fi < 1)
    def _():
        tr1[...] = jnp.zeros_like(tr1)

    @pl.when(fi < 2)
    def _():
        tr2[...] = jnp.zeros_like(tr2)

    def finish_rows(c):
        @pl.when(fi >= 1)
        def _():
            copy(("t1", c), ts1.at[c], tr1.at[c], (lax.rem(fi + 1, n_frame), ti)).wait_recv()

        @pl.when(fi >= 2)
        def _():
            copy(("t2", c), ts2.at[c], tr2.at[c], (lax.rem(fi + 2, n_frame), ti)).wait_recv()

        before_one = tr1[c].astype(jnp.float32)
        before_two = tr2[c].astype(jnp.float32)
        summed = now[c] + before_one[: 2 * dim] + before_two[: 2 * dim]
        squares = sq_own[c, 0:1, :] + before_one[2 * dim : 2 * dim + 1] + before_two[2 * dim : 2 * dim + 1]
        z = summed * lax.rsqrt(squares / (3 * width) + 1e-06)
        mixed = (0.5 * z * (1.0 + lax.erf(z * math.sqrt(0.5)))).astype(jnp.bfloat16)
        msend[c] = mixed[dim:]
        send(("mx", c), msend.at[c], mixbuf.at[2 * c + 1], tok(1))
        mixbuf[2 * c] = mixed[:dim]

    @pl.when(middle)
    def _():
        pass_on(3)

    mix_rows(0)

    @pl.when(middle)
    def _():
        pass_on(2)

    @pl.when(jnp.logical_not(middle))
    def _():
        for g in range(2):
            arrived(("lz", 1, g), lat_part(1, g), tok(2))

    mix_rows(1)

    @pl.when(jnp.logical_not(middle))
    def _():
        for g in range(2):
            arrived(("lz", 2, g), lat_part(2, g), tok(2))

    finish_rows(0)
    mix_rows(2)

    @pl.when(jnp.logical_not(middle))
    def _():
        for g in range(2):
            arrived(("lz", 3, g), lat_part(3, g), tok(2))

    mix_rows(3)
    for c in range(1, pairs):
        finish_rows(c)
    for k in range(n_tok):
        if k % 2:
            arrived(("mx", k // 2), mixbuf.at[k], tok(1))
        block = mixbuf[k]
        mix_t[:, k * rows : (k + 1) * rows] = block
        mix[k * rows : (k + 1) * rows, :] = block.T

    for k in range(1, n_tok):
        arrived(("oq", k), oqbuf.at[pl.ds(k * qrows, qrows), :], tok(k))
    for c in range(pairs - 1, -1, -1):
        q = oqbuf[2 * c * qrows : (2 * c + 2) * qrows, :]
        n, m, l = attend_columns(mix[...], mix_t[...], q, factor)
        o = (n / l).T
        for k in (2 * c, 2 * c + 1):
            part = o[(k - 2 * c) * qrows : (k - 2 * c + 1) * qrows]
            if k == 0:
                out_ref[0, :, own_cols] = part
            else:
                osend[k] = part.astype(jnp.bfloat16)
                send(("out", k), osend.at[k], obuf.at[k], tok(k))
    for k in range(n_tok - 1, 0, -1):
        arrived(("out", k), obuf.at[k], tok(k))
        cols = pl.ds(pl.multiple_of(peer[k] * dim, dim), dim)
        out_ref[0, :, cols] = obuf[k].astype(jnp.float32)

    for c in started:
        c.wait_send()

    @pl.when(middle)
    def _():
        for g in range(2):
            for slot in range(pairs):
                forward(slot, g).wait_send()

    for c in range(pairs):

        @pl.when(fi < n_frame - 1)
        def _():
            copy(("t1", c), ts1.at[c], tr1.at[c], (lax.rem(fi + 1, n_frame), ti)).wait_send()

        @pl.when(fi < n_frame - 2)
        def _():
            copy(("t2", c), ts2.at[c], tr2.at[c], (lax.rem(fi + 2, n_frame), ti)).wait_send()


def local_fused(inputs, kv_weight, latent_queries, mix_gain, mix_weight, output_queries):
    n_tok = lax.axis_size("tok")
    n_frame = lax.axis_size("frame")
    pairs = n_tok // 2
    heads = HEADS
    dim = HEAD_DIM
    width = heads * dim
    n_in = inputs.shape[1]
    rows = latent_queries.shape[0]
    qrows = output_queries.shape[1]
    bf16, f32 = jnp.bfloat16, jnp.float32
    stats = (pairs, 2, heads, rows)
    block = (pairs, heads, dim, rows)
    n_ids = len(copy_ids(n_tok, pairs))
    vmem = pltpu.VMEM
    scratch = [
        vmem((n_tok * rows, width), bf16),
        vmem((heads, n_in, dim), bf16),
        vmem((heads, dim, n_in), bf16),
        vmem((3 * width, dim), bf16),
        vmem((6 * dim, width), bf16),
        vmem(block, f32), vmem(stats, f32),
        vmem(block, bf16), vmem(stats, f32),
        vmem(block, bf16), vmem(stats, f32),
        vmem(block, bf16), vmem(stats, f32),
        vmem(block, bf16), vmem(stats, f32),
        vmem((pairs, width, rows), bf16),
        vmem((pairs, 2 * dim, rows), f32),
        vmem((pairs, 8, rows), f32),
        vmem((pairs, 2 * dim + 16, rows), bf16),
        vmem((pairs, 2 * dim + 16, rows), bf16),
        vmem((pairs, 2 * dim + 16, rows), bf16),
        vmem((pairs, 2 * dim + 16, rows), bf16),
        vmem((pairs, dim, rows), bf16),
        vmem((n_tok, dim, rows), bf16),
        vmem((dim, n_tok * rows), bf16),
        vmem((n_tok * rows, dim), bf16),
        vmem((n_tok * qrows, dim), bf16),
        vmem((n_tok, qrows, dim), bf16),
        vmem((n_tok, qrows, dim), bf16),
        pltpu.SemaphoreType.DMA((n_ids,)),
        pltpu.SemaphoreType.DMA((n_ids,)),
    ]
    return pl.pallas_call(
        functools.partial(window_kernel, n_tok, n_frame),
        out_shape=jax.ShapeDtypeStruct((1, qrows, width), f32),
        in_specs=[pl.BlockSpec(memory_space=pltpu.VMEM)] * 6,
        out_specs=pl.BlockSpec(memory_space=pltpu.VMEM),
        scratch_shapes=scratch,
        compiler_params=pltpu.CompilerParams(
            collective_id=0, has_side_effects=True, vmem_limit_bytes=56 * 1024 * 1024
        ),
    )(inputs, kv_weight, latent_queries, mix_gain, mix_weight, output_queries)


def pick_local(mesh):
    n_tok, n_frame = mesh.shape["tok"], mesh.shape["frame"]
    fits = n_tok == HEADS and n_frame % 2 == 0 and n_frame > 2
    return local_fused if fits else local


def solution(mesh):
    return jax.shard_map(
        pick_local(mesh),
        mesh=mesh,
        in_specs=(
            P("frame", "tok", None),
            P(),
            P("tok", None),
            P(),
            P(None, "tok"),
            P("frame", "tok", None),
        ),
        out_specs=P("frame", "tok", None),
        check_vma=False,
    )
```

```python
import functools
import math

import jax
import jax.numpy as jnp
from jax import lax
from jax.experimental import pallas as pl
from jax.experimental.pallas import tpu as pltpu
from jax.sharding import PartitionSpec as P

HEADS = 8
HEAD_DIM = 128


def from_behind(block, axis, distance):
    devices = range(lax.axis_size(axis))
    route = [(i - distance, i) for i in devices if i - distance in devices]
    return lax.ppermute(block, axis, route)


def attend_heads(queries, keys, values, head_count, head_dim):
    maxima = []
    numers = []
    denoms = []
    for head_index in range(head_count):
        low_col = head_index * head_dim
        high_col = low_col + head_dim
        scores = lax.dot_general(
            queries[:, low_col:high_col],
            keys[:, low_col:high_col],
            (((1,), (1,)), ((), ())),
            preferred_element_type=jnp.float32,
        ) / math.sqrt(head_dim)
        row_peak = jnp.max(scores, axis=1)
        weights = jnp.exp(scores - row_peak[:, None])
        denoms.append(jnp.sum(weights, axis=1))
        numers.append(
            jnp.dot(
                weights.astype(jnp.bfloat16),
                values[:, low_col:high_col],
                preferred_element_type=jnp.float32,
            )
        )
        maxima.append(row_peak)
    return (jnp.stack(maxima, axis=1), jnp.concatenate(numers, axis=1), jnp.stack(denoms, axis=1))


def finish_latents(numerator, denominator, head_count, head_dim):
    row_count = numerator.shape[0]
    shaped = numerator.reshape(row_count, head_count, head_dim) / denominator[:, :, None]
    return shaped.reshape(row_count, head_count * head_dim).astype(jnp.bfloat16)


def project_cols(latent_part, gain_part, weight_part):
    scaled = (latent_part.astype(jnp.float32) * gain_part).astype(jnp.bfloat16)
    return lax.dot_general(
        weight_part, scaled, (((0,), (1,)), ((), ())), preferred_element_type=jnp.float32
    )


def local(inputs, kv_weight, latent_queries, mix_gain, mix_weight, output_queries):
    head_count = HEADS
    head_dim = HEAD_DIM
    latent_width = head_count * head_dim
    frame_inputs = inputs[0]
    queries = lax.all_gather(latent_queries, "tok", axis=0, tiled=True)
    key_values = jnp.dot(frame_inputs, kv_weight, preferred_element_type=jnp.float32).astype(
        jnp.bfloat16
    )
    maxima, numers, denoms = attend_heads(
        queries, key_values[:, :latent_width], key_values[:, latent_width:], head_count, head_dim
    )
    peak_all = lax.pmax(maxima.astype(jnp.bfloat16), "tok").astype(maxima.dtype)
    rescale = jnp.exp(maxima - peak_all)
    latent_count = queries.shape[0]
    numer_terms = (
        numers.reshape(latent_count, head_count, head_dim) * rescale[:, :, None]
    ).reshape(latent_count, latent_width)
    denom_terms = denoms * rescale
    numerator, denominator = (
        lax.psum(numer_terms.astype(jnp.bfloat16), "tok").astype(jnp.float32),
        lax.psum(denom_terms.astype(jnp.bfloat16), "tok").astype(jnp.float32),
    )
    latents = finish_latents(numerator, denominator, head_count, head_dim)
    latent_f32 = latents.astype(jnp.float32)
    own_squares = jnp.sum(latent_f32 * latent_f32, axis=1)
    term_now = project_cols(latents, mix_gain[:latent_width], mix_weight[:latent_width])
    term_one, squares_one = (
        from_behind(
            project_cols(
                latents,
                mix_gain[latent_width : 2 * latent_width],
                mix_weight[latent_width : 2 * latent_width],
            ).astype(jnp.bfloat16),
            "frame",
            1,
        ).astype(jnp.float32),
        from_behind(own_squares.astype(jnp.bfloat16), "frame", 1).astype(own_squares.dtype),
    )
    term_two, squares_two = (
        from_behind(
            project_cols(
                latents, mix_gain[2 * latent_width :], mix_weight[2 * latent_width :]
            ).astype(jnp.bfloat16),
            "frame",
            2,
        ).astype(jnp.float32),
        from_behind(own_squares.astype(jnp.bfloat16), "frame", 2).astype(own_squares.dtype),
    )
    summed = term_now + term_one + term_two
    squares = own_squares + squares_one + squares_two
    inverse = lax.rsqrt(squares / (3 * latent_width) + 1e-06)
    mixed_cols = jax.nn.gelu(summed * inverse[None, :], approximate=False).astype(jnp.bfloat16)
    mixed_t = lax.all_gather(mixed_cols, "tok", axis=0, tiled=True)
    frame_queries = output_queries[0]
    pieces = []
    for head_index in range(head_count):
        low_col = head_index * head_dim
        high_col = low_col + head_dim
        scores = jnp.dot(
            frame_queries[:, low_col:high_col],
            mixed_t[low_col:high_col],
            preferred_element_type=jnp.float32,
        ) / math.sqrt(head_dim)
        row_peak = jnp.max(scores, axis=1)
        weights = jnp.exp(scores - row_peak[:, None])
        denom_sum = jnp.sum(weights, axis=1)
        head_sum = lax.dot_general(
            weights.astype(jnp.bfloat16),
            mixed_t[low_col:high_col],
            (((1,), (1,)), ((), ())),
            preferred_element_type=jnp.float32,
        )
        pieces.append(head_sum / denom_sum[:, None])
    result = jnp.concatenate(pieces, axis=1)
    return result[None]


MESH = pl.DeviceIdType.MESH
LOG2E = 1.4426950408889634
ONES = 16


def dot_nt(a, b):
    return lax.dot_general(a, b, (((1,), (1,)), ((), ())), preferred_element_type=jnp.float32)


def attend_units(units, finish):
    def score(unit):
        keys, _, queries, factor = unit()
        scores = dot_nt(keys, queries)
        return scores if factor is None else scores * factor

    ahead = score(units[0])
    for i, unit in enumerate(units):
        scores = ahead
        if i + 1 < len(units):
            ahead = score(units[i + 1])
        peak = jnp.max(scores, axis=0, keepdims=True)
        weights = jnp.exp2(scores - peak).astype(jnp.bfloat16)
        values = unit()[1]
        numer = jnp.dot(values, weights, preferred_element_type=jnp.float32)
        dim = values.shape[0] - ONES
        finish(i, numer[:dim], peak, numer[dim : dim + 1])


def copy_ids(n_tok, pairs):
    names = []
    for j in range(1, pairs):
        names += [("qz", j), ("qx", j)]
    for j in range(pairs):
        names += [("t1", j), ("t2", j), ("mx", j)]
        for g in range(2):
            names += [(n, j, g) for n in ("nx", "sx", "nz", "sz", "lz", "fz")]
    for k in range(1, n_tok):
        names += [("qc", k), ("oq", k), ("out", k)]
    names += [("qx", 0), ("wx",), ("wc",)]
    return {name: i for i, name in enumerate(names)}


def window_kernel(
    n_tok, n_frame, x_ref, kvw_ref, lq_ref, gain_ref, w_ref, oq_ref, out_ref,
    qbuf, kbuf, vbuf, wbuf, w3, own_n, own_s, xs_n, xs_s, xr_n, xr_s, zs_n, zs_s, zr_n, zr_s,
    lat, now, sq_own, ts1, ts2, tr1, tr2, msend, mixbuf, mix_t, mix, oqbuf, osend, obuf, send_sem, recv_sem,
):
    heads = n_tok
    pairs = n_tok // 2
    rows = lq_ref.shape[0]
    dim = w_ref.shape[1]
    width = heads * dim
    qrows = oq_ref.shape[1]
    factor = LOG2E / math.sqrt(dim)
    ids = copy_ids(n_tok, pairs)
    fi = lax.axis_index("frame")
    ti = lax.axis_index("tok")
    half = rows // 2
    mine = lax.rem(fi, 2)
    sibling = fi + 1 - 2 * mine
    started = []

    def flip(k):
        out = 0
        bit = 1
        while bit < n_tok:
            b = lax.rem(lax.div(ti, bit), 2)
            out = out + bit * ((1 - b) if (k & bit) else b)
            bit *= 2
        return out

    peer = [flip(k) for k in range(n_tok)]

    def copy(name, src, dst, where, send_name=None):
        return pltpu.make_async_remote_copy(
            src_ref=src, dst_ref=dst,
            send_sem=send_sem.at[ids[send_name or name]], recv_sem=recv_sem.at[ids[name]],
            device_id=where, device_id_type=MESH,
        )

    def send(name, src, dst, where):
        c = copy(name, src, dst, where)
        c.start()
        started.append(c)

    def arrived(name, dst, where):
        copy(name, dst, dst, where).wait_recv()

    def tok(k):
        return (fi, peer[k])

    barrier = pltpu.get_barrier_semaphore()
    for k in range(1, n_tok):
        pl.semaphore_signal(barrier, inc=1, device_id=tok(k), device_id_type=MESH)
    for o in range(1, n_frame):
        pl.semaphore_signal(
            barrier, inc=1, device_id=(lax.rem(fi + o, n_frame), ti), device_id_type=MESH
        )
    pl.semaphore_wait(barrier, n_tok - 1 + n_frame - 1)

    here = pl.multiple_of(mine * half, half)
    there = pl.multiple_of((1 - mine) * half, half)

    def qpart(k, off):
        return qbuf.at[pl.ds(k * rows + off, half), :]

    own_half = lq_ref.at[pl.ds(here, half), :]
    for j in range(pairs - 1, 0, -1):
        send(("qz", j), own_half, qpart(2 * j, here), tok(2 * j))
    send(("qx", 0), own_half, qpart(1, here), tok(1))
    qbuf[0:rows, :] = lq_ref[...]
    own_cols = pl.ds(pl.multiple_of(ti * dim, dim), dim)
    oqbuf[0:qrows, :] = oq_ref[0, :, own_cols]

    def project_keys(i, carry):
        cols = pl.ds(pl.multiple_of(i * 2 * dim, 2 * dim), 2 * dim)
        k = jnp.dot(x_ref[0], kvw_ref[:, cols], preferred_element_type=jnp.float32)
        k = (k * factor).astype(jnp.bfloat16)
        kbuf[2 * i] = k[:, :dim]
        kbuf[2 * i + 1] = k[:, dim:]
        return carry

    lax.fori_loop(0, heads // 2, project_keys, 0, unroll=True)

    arrived(("qx", 0), qpart(1, here), tok(1))
    send(("qc", 1), qpart(1, here), qpart(1, here), (sibling, ti))
    def project_values(i, carry):
        cols = pl.ds(pl.multiple_of(width + i * 2 * dim, 2 * dim), 2 * dim)
        v = jnp.dot(x_ref[0], kvw_ref[:, cols], preferred_element_type=jnp.float32)
        v = v.astype(jnp.bfloat16).T
        vbuf[2 * i, 0:dim, :] = v[:dim]
        vbuf[2 * i + 1, 0:dim, :] = v[dim:]
        return carry

    vbuf[:, dim:, :] = jnp.ones((heads, ONES, vbuf.shape[2]), jnp.bfloat16)
    lax.fori_loop(0, heads // 2, project_values, 0, unroll=True)

    group = heads // 2

    def heads_of(g):
        return pl.ds(g * group, group)

    def merge_x(j, g):
        arrived(("nx", j, g), xr_n.at[j, heads_of(g)], tok(1))
        arrived(("sx", j, g), xr_s.at[j, g], tok(1))
        m1, l1 = own_s[j, g, 0:group, :], own_s[j, g, group:, :]
        m2, l2 = xr_s[j, g, 0:group, :], xr_s[j, g, group:, :]
        m = jnp.maximum(m1, m2)
        a1, a2 = jnp.exp2(m1 - m), jnp.exp2(m2 - m)
        target = own_s if j == 0 else zs_s
        target[j, g, 0:group, :] = m
        target[j, g, group:, :] = l1 * a1 + l2 * a2
        for i in range(group):
            h = g * group + i
            n = own_n[j, h] * a1[i : i + 1] + xr_n[j, h].astype(jnp.float32) * a2[i : i + 1]
            if j == 0:
                own_n[0, h] = n
            else:
                zs_n[j, h] = n.astype(jnp.bfloat16)
        if j > 0:
            where = tok(2 * j)
            send(("nz", j, g), zs_n.at[j, heads_of(g)], zr_n.at[j, heads_of(g)], where)
            send(("sz", j, g), zs_s.at[j, g], zr_s.at[j, g], where)

    def attend_unit(j, g):
        def unit(r):
            h = g * group + r
            q = qbuf[2 * j * rows : (2 * j + 2) * rows, h * dim : (h + 1) * dim]
            return kbuf[h], vbuf[h], q, None

        def finish(r, n, m, l):
            h = g * group + r
            own_n[j, h] = n[:, :rows]
            own_s[j, g, r : r + 1, :] = m[:, :rows]
            own_s[j, g, group + r : group + r + 1, :] = l[:, :rows]
            xs_n[j, h] = n[:, rows:].astype(jnp.bfloat16)
            xs_s[j, g, r : r + 1, :] = m[:, rows:]
            xs_s[j, g, group + r : group + r + 1, :] = l[:, rows:]

        attend_units([functools.partial(unit, r) for r in range(group)], finish)
        send(("nx", j, g), xs_n.at[j, heads_of(g)], xr_n.at[j, heads_of(g)], tok(1))
        send(("sx", j, g), xs_s.at[j, g], xr_s.at[j, g], tok(1))

    def wait_queries(j):
        for k in (2 * j, 2 * j + 1):
            if k > 0:
                arrived(("qc", k), qpart(k, there), (sibling, ti))

    wait_queries(0)
    attend_unit(0, 0)
    for j in range(pairs - 1, 0, -1):
        arrived(("qz", j), qpart(2 * j, here), tok(2 * j))
        send(("qx", j), qpart(2 * j, here), qpart(2 * j + 1, here), tok(1))
        send(("qc", 2 * j), qpart(2 * j, here), qpart(2 * j, here), (sibling, ti))
    attend_unit(0, 1)
    merge_x(0, 0)
    for j in range(pairs - 1, 0, -1):
        k = 2 * j + 1
        arrived(("qx", j), qpart(k, here), tok(1))
        send(("qc", k), qpart(k, here), qpart(k, here), (sibling, ti))
    for k in range(n_tok - 1, 0, -1):
        cols = pl.ds(pl.multiple_of(peer[k] * dim, dim), dim)
        send(("oq", k), oq_ref.at[0, :, cols], oqbuf.at[pl.ds(k * qrows, qrows), :], tok(k))
    before = (0, 1)
    for j in range(pairs - 1, 0, -1):
        wait_queries(j)
        for g in range(2):
            attend_unit(j, g)
            merge_x(*before)
            before = (j, g)
    w_rows = w_ref.shape[0] // 2
    w_here = pl.ds(pl.multiple_of(mine * w_rows, w_rows), w_rows)
    w_there = pl.ds(pl.multiple_of((1 - mine) * w_rows, w_rows), w_rows)
    send(("wx",), w_ref.at[w_here, :], wbuf.at[w_here, :], tok(1))
    merge_x(*before)

    line = lax.div(ti, 2)
    middle = jnp.logical_and(line > 0, line < pairs - 1)

    def lat_part(slot, g):
        return lat.at[slot, pl.ds(g * group * dim, group * dim), :]

    def forward(slot, g):
        far, near = tok(2 * (pairs - 1)), tok(2)
        plan = {0: (3, far), 1: (2, far), 3: (2, near), 2: (3, near)}
        there_slot, where = plan[slot]
        return copy(
            ("lz", there_slot, g), lat_part(slot, g), lat_part(there_slot, g), where, ("fz", slot, g)
        )

    def pass_on(slot):
        for g in range(2):
            arrived(("lz", slot, g), lat_part(slot, g), tok(2))
            forward(slot, g).start()

    for g in range(2):
        for j in range(pairs - 1, 0, -1):
            arrived(("nz", j, g), zr_n.at[j, heads_of(g)], tok(2 * j))
            arrived(("sz", j, g), zr_s.at[j, g], tok(2 * j))
        peaks = [own_s[0, g, 0:group, :]] + [zr_s[j, g, 0:group, :] for j in range(1, pairs)]
        dens = [own_s[0, g, group:, :]] + [zr_s[j, g, group:, :] for j in range(1, pairs)]
        top = functools.reduce(jnp.maximum, peaks)
        scale = [jnp.exp2(p - top) for p in peaks]
        total = sum(d * s for d, s in zip(dens, scale))
        scale = [s / total for s in scale]
        for i in range(group):
            h = g * group + i
            n = own_n[0, h] * scale[0][i : i + 1]
            for j in range(1, pairs):
                n = n + zr_n[j, h].astype(jnp.float32) * scale[j][i : i + 1]
            lat[0, h * dim : (h + 1) * dim, :] = n.astype(jnp.bfloat16)
        send(("lz", 1, g), lat_part(0, g), lat_part(1, g), tok(2))

        @pl.when(middle)
        def _():
            forward(0, g).start()

    def mix_weights(source, place):
        for t in range(3):
            w_t = source[t * width : (t + 1) * width, :].T.astype(jnp.float32)
            gain = gain_ref[t * width : (t + 1) * width].reshape(1, width)
            at = 2 * t + place
            w3[at * dim : (at + 1) * dim, :] = (w_t * gain).astype(jnp.bfloat16)

    arrived(("wx",), wbuf.at[w_here, :], tok(1))
    send(("wc",), wbuf.at[w_here, :], wbuf.at[w_here, :], (sibling, ti))
    mix_weights(w_ref, 0)

    @pl.when(middle)
    def _():
        pass_on(1)

    arrived(("wc",), wbuf.at[w_there, :], (sibling, ti))
    mix_weights(wbuf, 1)

    def mix_rows(c):
        block = lat[c]
        wide = block.astype(jnp.float32)
        squares = jnp.sum(wide * wide, axis=0, keepdims=True)
        terms = jnp.dot(w3[...], block, preferred_element_type=jnp.float32)
        now[c] = terms[: 2 * dim]
        sq_own[c] = jnp.broadcast_to(squares, sq_own.shape[1:])
        sq = jnp.broadcast_to(squares, (16, rows)).astype(jnp.bfloat16)
        ts1[c, 0 : 2 * dim, :] = terms[2 * dim : 4 * dim].astype(jnp.bfloat16)
        ts1[c, 2 * dim :, :] = sq
        ts2[c, 0 : 2 * dim, :] = terms[4 * dim :].astype(jnp.bfloat16)
        ts2[c, 2 * dim :, :] = sq

        @pl.when(fi < n_frame - 1)
        def _():
            copy(("t1", c), ts1.at[c], tr1.at[c], (lax.rem(fi + 1, n_frame), ti)).start()

        @pl.when(fi < n_frame - 2)
        def _():
            copy(("t2", c), ts2.at[c], tr2.at[c], (lax.rem(fi + 2, n_frame), ti)).start()

    @pl.when(fi < 1)
    def _():
        tr1[...] = jnp.zeros_like(tr1)

    @pl.when(fi < 2)
    def _():
        tr2[...] = jnp.zeros_like(tr2)

    def finish_rows(c):
        @pl.when(fi >= 1)
        def _():
            copy(("t1", c), ts1.at[c], tr1.at[c], (lax.rem(fi + 1, n_frame), ti)).wait_recv()

        @pl.when(fi >= 2)
        def _():
            copy(("t2", c), ts2.at[c], tr2.at[c], (lax.rem(fi + 2, n_frame), ti)).wait_recv()

        before_one = tr1[c].astype(jnp.float32)
        before_two = tr2[c].astype(jnp.float32)
        summed = now[c] + before_one[: 2 * dim] + before_two[: 2 * dim]
        squares = sq_own[c, 0:1, :] + before_one[2 * dim : 2 * dim + 1] + before_two[2 * dim : 2 * dim + 1]
        z = summed * lax.rsqrt(squares / (3 * width) + 1e-06)
        mixed = (0.5 * z * (1.0 + lax.erf(z * math.sqrt(0.5)))).astype(jnp.bfloat16)
        msend[c] = mixed[dim:]
        send(("mx", c), msend.at[c], mixbuf.at[2 * c + 1], tok(1))
        mixbuf[2 * c] = mixed[:dim]

    @pl.when(middle)
    def _():
        pass_on(3)

    mix_rows(0)

    @pl.when(middle)
    def _():
        pass_on(2)

    @pl.when(jnp.logical_not(middle))
    def _():
        for g in range(2):
            arrived(("lz", 1, g), lat_part(1, g), tok(2))

    mix_rows(1)

    @pl.when(jnp.logical_not(middle))
    def _():
        for g in range(2):
            arrived(("lz", 2, g), lat_part(2, g), tok(2))

    finish_rows(0)
    mix_rows(2)

    @pl.when(jnp.logical_not(middle))
    def _():
        for g in range(2):
            arrived(("lz", 3, g), lat_part(3, g), tok(2))

    mix_rows(3)
    for c in range(1, pairs):
        finish_rows(c)
    for k in range(n_tok):
        if k % 2:
            arrived(("mx", k // 2), mixbuf.at[k], tok(1))
        block = mixbuf[k]
        mix_t[0:dim, k * rows : (k + 1) * rows] = block
        mix[k * rows : (k + 1) * rows, :] = block.T

    for k in range(1, n_tok):
        arrived(("oq", k), oqbuf.at[pl.ds(k * qrows, qrows), :], tok(k))
    mix_t[dim:, :] = jnp.ones((ONES, mix_t.shape[1]), jnp.bfloat16)

    def decode_unit(i):
        c = pairs - 1 - i
        return mix[...], mix_t[...], oqbuf[2 * c * qrows : (2 * c + 2) * qrows, :], factor

    def decode_finish(i, n, m, l):
        c = pairs - 1 - i
        o = (n / l).T
        for k in (2 * c, 2 * c + 1):
            part = o[(k - 2 * c) * qrows : (k - 2 * c + 1) * qrows]
            if k == 0:
                out_ref[0, :, own_cols] = part
            else:
                osend[k] = part.astype(jnp.bfloat16)
                send(("out", k), osend.at[k], obuf.at[k], tok(k))

    attend_units([functools.partial(decode_unit, i) for i in range(pairs)], decode_finish)
    for k in range(n_tok - 1, 0, -1):
        arrived(("out", k), obuf.at[k], tok(k))
        cols = pl.ds(pl.multiple_of(peer[k] * dim, dim), dim)
        out_ref[0, :, cols] = obuf[k].astype(jnp.float32)

    for c in started:
        c.wait_send()

    @pl.when(middle)
    def _():
        for g in range(2):
            for slot in range(pairs):
                forward(slot, g).wait_send()

    for c in range(pairs):

        @pl.when(fi < n_frame - 1)
        def _():
            copy(("t1", c), ts1.at[c], tr1.at[c], (lax.rem(fi + 1, n_frame), ti)).wait_send()

        @pl.when(fi < n_frame - 2)
        def _():
            copy(("t2", c), ts2.at[c], tr2.at[c], (lax.rem(fi + 2, n_frame), ti)).wait_send()


def local_fused(inputs, kv_weight, latent_queries, mix_gain, mix_weight, output_queries):
    n_tok = lax.axis_size("tok")
    n_frame = lax.axis_size("frame")
    pairs = n_tok // 2
    heads = HEADS
    dim = HEAD_DIM
    width = heads * dim
    n_in = inputs.shape[1]
    rows = latent_queries.shape[0]
    qrows = output_queries.shape[1]
    bf16, f32 = jnp.bfloat16, jnp.float32
    stats = (pairs, 2, heads, rows)
    block = (pairs, heads, dim, rows)
    n_ids = len(copy_ids(n_tok, pairs))
    vmem = pltpu.VMEM
    scratch = [
        vmem((n_tok * rows, width), bf16),
        vmem((heads, n_in, dim), bf16),
        vmem((heads, dim + ONES, n_in), bf16),
        vmem((3 * width, dim), bf16),
        vmem((6 * dim, width), bf16),
        vmem(block, f32), vmem(stats, f32),
        vmem(block, bf16), vmem(stats, f32),
        vmem(block, bf16), vmem(stats, f32),
        vmem(block, bf16), vmem(stats, f32),
        vmem(block, bf16), vmem(stats, f32),
        vmem((pairs, width, rows), bf16),
        vmem((pairs, 2 * dim, rows), f32),
        vmem((pairs, 8, rows), f32),
        vmem((pairs, 2 * dim + 16, rows), bf16),
        vmem((pairs, 2 * dim + 16, rows), bf16),
        vmem((pairs, 2 * dim + 16, rows), bf16),
        vmem((pairs, 2 * dim + 16, rows), bf16),
        vmem((pairs, dim, rows), bf16),
        vmem((n_tok, dim, rows), bf16),
        vmem((dim + ONES, n_tok * rows), bf16),
        vmem((n_tok * rows, dim), bf16),
        vmem((n_tok * qrows, dim), bf16),
        vmem((n_tok, qrows, dim), bf16),
        vmem((n_tok, qrows, dim), bf16),
        pltpu.SemaphoreType.DMA((n_ids,)),
        pltpu.SemaphoreType.DMA((n_ids,)),
    ]
    return pl.pallas_call(
        functools.partial(window_kernel, n_tok, n_frame),
        out_shape=jax.ShapeDtypeStruct((1, qrows, width), f32),
        in_specs=[pl.BlockSpec(memory_space=pltpu.VMEM)] * 6,
        out_specs=pl.BlockSpec(memory_space=pltpu.VMEM),
        scratch_shapes=scratch,
        compiler_params=pltpu.CompilerParams(
            collective_id=0, has_side_effects=True, vmem_limit_bytes=56 * 1024 * 1024
        ),
    )(inputs, kv_weight, latent_queries, mix_gain, mix_weight, output_queries)


def pick_local(mesh):
    n_tok, n_frame = mesh.shape["tok"], mesh.shape["frame"]
    fits = n_tok == HEADS and n_frame % 2 == 0 and n_frame > 2
    return local_fused if fits else local


def solution(mesh):
    return jax.shard_map(
        pick_local(mesh),
        mesh=mesh,
        in_specs=(
            P("frame", "tok", None),
            P(),
            P("tok", None),
            P(),
            P(None, "tok"),
            P("frame", "tok", None),
        ),
        out_specs=P("frame", "tok", None),
        check_vma=False,
    )
```

```python
import functools
import math

import jax
import jax.numpy as jnp
from jax import lax
from jax.experimental import pallas as pl
from jax.experimental.pallas import tpu as pltpu
from jax.sharding import PartitionSpec as P

HEADS = 8
HEAD_DIM = 128


def from_behind(block, axis, distance):
    devices = range(lax.axis_size(axis))
    route = [(i - distance, i) for i in devices if i - distance in devices]
    return lax.ppermute(block, axis, route)


def attend_heads(queries, keys, values, head_count, head_dim):
    maxima = []
    numers = []
    denoms = []
    for head_index in range(head_count):
        low_col = head_index * head_dim
        high_col = low_col + head_dim
        scores = lax.dot_general(
            queries[:, low_col:high_col],
            keys[:, low_col:high_col],
            (((1,), (1,)), ((), ())),
            preferred_element_type=jnp.float32,
        ) / math.sqrt(head_dim)
        row_peak = jnp.max(scores, axis=1)
        weights = jnp.exp(scores - row_peak[:, None])
        denoms.append(jnp.sum(weights, axis=1))
        numers.append(
            jnp.dot(
                weights.astype(jnp.bfloat16),
                values[:, low_col:high_col],
                preferred_element_type=jnp.float32,
            )
        )
        maxima.append(row_peak)
    return (jnp.stack(maxima, axis=1), jnp.concatenate(numers, axis=1), jnp.stack(denoms, axis=1))


def finish_latents(numerator, denominator, head_count, head_dim):
    row_count = numerator.shape[0]
    shaped = numerator.reshape(row_count, head_count, head_dim) / denominator[:, :, None]
    return shaped.reshape(row_count, head_count * head_dim).astype(jnp.bfloat16)


def project_cols(latent_part, gain_part, weight_part):
    scaled = (latent_part.astype(jnp.float32) * gain_part).astype(jnp.bfloat16)
    return lax.dot_general(
        weight_part, scaled, (((0,), (1,)), ((), ())), preferred_element_type=jnp.float32
    )


def local(inputs, kv_weight, latent_queries, mix_gain, mix_weight, output_queries):
    head_count = HEADS
    head_dim = HEAD_DIM
    latent_width = head_count * head_dim
    frame_inputs = inputs[0]
    queries = lax.all_gather(latent_queries, "tok", axis=0, tiled=True)
    key_values = jnp.dot(frame_inputs, kv_weight, preferred_element_type=jnp.float32).astype(
        jnp.bfloat16
    )
    maxima, numers, denoms = attend_heads(
        queries, key_values[:, :latent_width], key_values[:, latent_width:], head_count, head_dim
    )
    peak_all = lax.pmax(maxima.astype(jnp.bfloat16), "tok").astype(maxima.dtype)
    rescale = jnp.exp(maxima - peak_all)
    latent_count = queries.shape[0]
    numer_terms = (
        numers.reshape(latent_count, head_count, head_dim) * rescale[:, :, None]
    ).reshape(latent_count, latent_width)
    denom_terms = denoms * rescale
    numerator, denominator = (
        lax.psum(numer_terms.astype(jnp.bfloat16), "tok").astype(jnp.float32),
        lax.psum(denom_terms.astype(jnp.bfloat16), "tok").astype(jnp.float32),
    )
    latents = finish_latents(numerator, denominator, head_count, head_dim)
    latent_f32 = latents.astype(jnp.float32)
    own_squares = jnp.sum(latent_f32 * latent_f32, axis=1)
    term_now = project_cols(latents, mix_gain[:latent_width], mix_weight[:latent_width])
    term_one, squares_one = (
        from_behind(
            project_cols(
                latents,
                mix_gain[latent_width : 2 * latent_width],
                mix_weight[latent_width : 2 * latent_width],
            ).astype(jnp.bfloat16),
            "frame",
            1,
        ).astype(jnp.float32),
        from_behind(own_squares.astype(jnp.bfloat16), "frame", 1).astype(own_squares.dtype),
    )
    term_two, squares_two = (
        from_behind(
            project_cols(
                latents, mix_gain[2 * latent_width :], mix_weight[2 * latent_width :]
            ).astype(jnp.bfloat16),
            "frame",
            2,
        ).astype(jnp.float32),
        from_behind(own_squares.astype(jnp.bfloat16), "frame", 2).astype(own_squares.dtype),
    )
    summed = term_now + term_one + term_two
    squares = own_squares + squares_one + squares_two
    inverse = lax.rsqrt(squares / (3 * latent_width) + 1e-06)
    mixed_cols = jax.nn.gelu(summed * inverse[None, :], approximate=False).astype(jnp.bfloat16)
    mixed_t = lax.all_gather(mixed_cols, "tok", axis=0, tiled=True)
    frame_queries = output_queries[0]
    pieces = []
    for head_index in range(head_count):
        low_col = head_index * head_dim
        high_col = low_col + head_dim
        scores = jnp.dot(
            frame_queries[:, low_col:high_col],
            mixed_t[low_col:high_col],
            preferred_element_type=jnp.float32,
        ) / math.sqrt(head_dim)
        row_peak = jnp.max(scores, axis=1)
        weights = jnp.exp(scores - row_peak[:, None])
        denom_sum = jnp.sum(weights, axis=1)
        head_sum = lax.dot_general(
            weights.astype(jnp.bfloat16),
            mixed_t[low_col:high_col],
            (((1,), (1,)), ((), ())),
            preferred_element_type=jnp.float32,
        )
        pieces.append(head_sum / denom_sum[:, None])
    result = jnp.concatenate(pieces, axis=1)
    return result[None]


MESH = pl.DeviceIdType.MESH
LOG2E = 1.4426950408889634
ONES = 16


def dot_nt(a, b):
    return lax.dot_general(a, b, (((1,), (1,)), ((), ())), preferred_element_type=jnp.float32)


def attend_units(units, finish):
    def score(unit):
        keys, _, queries, factor = unit()
        scores = dot_nt(keys, queries)
        return scores if factor is None else scores * factor

    ahead = score(units[0])
    for i, unit in enumerate(units):
        scores = ahead
        if i + 1 < len(units):
            ahead = score(units[i + 1])
        peak = jnp.max(scores, axis=0, keepdims=True)
        weights = jnp.exp2(scores - peak).astype(jnp.bfloat16)
        values = unit()[1]
        numer = jnp.dot(values, weights, preferred_element_type=jnp.float32)
        dim = values.shape[0] - ONES
        finish(i, numer[:dim], peak, numer[dim : dim + 1])


def copy_ids(n_tok, pairs):
    names = []
    for j in range(1, pairs):
        names += [("qz", j), ("qx", j)]
    for j in range(pairs):
        names += [("t1", j), ("t2", j), ("mx", j)]
        for g in range(2):
            names += [(n, j, g) for n in ("nx", "sx", "nz", "sz", "lz", "fz")]
    for k in range(1, n_tok):
        names += [("qc", k), ("qy", k), ("oq", k), ("out", k)]
    names += [("qx", 0), ("wx",), ("wc",)]
    return {name: i for i, name in enumerate(names)}


def window_kernel(
    n_tok, n_frame, x_ref, kvw_ref, lq_ref, gain_ref, w_ref, oq_ref, out_ref,
    qbuf, kbuf, vbuf, wbuf, w3, own_n, own_s, xs_n, xs_s, xr_n, xr_s, zs_n, zs_s, zr_n, zr_s,
    lat, now, sq_own, ts1, ts2, tr1, tr2, msend, mixbuf, mix_t, mix, oqbuf, osend, obuf, send_sem, recv_sem,
):
    heads = n_tok
    pairs = n_tok // 2
    rows = lq_ref.shape[0]
    dim = w_ref.shape[1]
    width = heads * dim
    qrows = oq_ref.shape[1]
    factor = LOG2E / math.sqrt(dim)
    ids = copy_ids(n_tok, pairs)
    fi = lax.axis_index("frame")
    ti = lax.axis_index("tok")
    half = rows // 2
    mine = lax.rem(fi, 2)
    sibling = fi + 1 - 2 * mine
    started = []

    def flip(k):
        out = 0
        bit = 1
        while bit < n_tok:
            b = lax.rem(lax.div(ti, bit), 2)
            out = out + bit * ((1 - b) if (k & bit) else b)
            bit *= 2
        return out

    peer = [flip(k) for k in range(n_tok)]

    def copy(name, src, dst, where, send_name=None):
        return pltpu.make_async_remote_copy(
            src_ref=src, dst_ref=dst,
            send_sem=send_sem.at[ids[send_name or name]], recv_sem=recv_sem.at[ids[name]],
            device_id=where, device_id_type=MESH,
        )

    def send(name, src, dst, where):
        c = copy(name, src, dst, where)
        c.start()
        started.append(c)

    def arrived(name, dst, where):
        copy(name, dst, dst, where).wait_recv()

    def tok(k):
        return (fi, peer[k])

    barrier = pltpu.get_barrier_semaphore()
    for k in range(1, n_tok):
        pl.semaphore_signal(barrier, inc=1, device_id=tok(k), device_id_type=MESH)
    for o in range(1, n_frame):
        pl.semaphore_signal(
            barrier, inc=1, device_id=(lax.rem(fi + o, n_frame), ti), device_id_type=MESH
        )
    pl.semaphore_wait(barrier, n_tok - 1 + n_frame - 1)

    here = pl.multiple_of(mine * half, half)
    there = pl.multiple_of((1 - mine) * half, half)

    quarter = half // 2
    plane = lax.rem(lax.div(fi, 2), 2)
    across = fi + 2 - 4 * plane
    near_rows = pl.multiple_of(here + plane * quarter, quarter)
    far_rows = pl.multiple_of(here + (1 - plane) * quarter, quarter)

    def qpart(k, off, count=half):
        return qbuf.at[pl.ds(k * rows + off, count), :]

    def qnear(k):
        return qpart(k, near_rows, quarter)

    def send_across(k):
        send(("qy", k), qnear(k), qnear(k), (across, ti))

    def send_sibling(k):
        arrived(("qy", k), qpart(k, far_rows, quarter), (across, ti))
        send(("qc", k), qpart(k, here), qpart(k, here), (sibling, ti))

    own_part = lq_ref.at[pl.ds(near_rows, quarter), :]
    for j in range(pairs - 1, 0, -1):
        send(("qz", j), own_part, qnear(2 * j), tok(2 * j))
    send(("qx", 0), own_part, qnear(1), tok(1))
    qbuf[0:rows, :] = lq_ref[...]
    own_cols = pl.ds(pl.multiple_of(ti * dim, dim), dim)
    oqbuf[0:qrows, :] = oq_ref[0, :, own_cols]

    def project_keys(i, carry):
        cols = pl.ds(pl.multiple_of(i * 2 * dim, 2 * dim), 2 * dim)
        k = jnp.dot(x_ref[0], kvw_ref[:, cols], preferred_element_type=jnp.float32)
        k = (k * factor).astype(jnp.bfloat16)
        kbuf[2 * i] = k[:, :dim]
        kbuf[2 * i + 1] = k[:, dim:]
        return carry

    lax.fori_loop(0, heads // 2, project_keys, 0, unroll=True)

    arrived(("qx", 0), qnear(1), tok(1))
    send_across(1)
    def project_values(i, carry):
        cols = pl.ds(pl.multiple_of(width + i * 2 * dim, 2 * dim), 2 * dim)
        v = jnp.dot(x_ref[0], kvw_ref[:, cols], preferred_element_type=jnp.float32)
        v = v.astype(jnp.bfloat16).T
        vbuf[2 * i, 0:dim, :] = v[:dim]
        vbuf[2 * i + 1, 0:dim, :] = v[dim:]
        return carry

    vbuf[:, dim:, :] = jnp.ones((heads, ONES, vbuf.shape[2]), jnp.bfloat16)
    lax.fori_loop(0, heads // 2, project_values, 0, unroll=True)

    group = heads // 2

    def heads_of(g):
        return pl.ds(g * group, group)

    def merge_x(j, g):
        arrived(("nx", j, g), xr_n.at[j, heads_of(g)], tok(1))
        arrived(("sx", j, g), xr_s.at[j, g], tok(1))
        m1, l1 = own_s[j, g, 0:group, :], own_s[j, g, group:, :]
        m2, l2 = xr_s[j, g, 0:group, :], xr_s[j, g, group:, :]
        m = jnp.maximum(m1, m2)
        a1, a2 = jnp.exp2(m1 - m), jnp.exp2(m2 - m)
        target = own_s if j == 0 else zs_s
        target[j, g, 0:group, :] = m
        target[j, g, group:, :] = l1 * a1 + l2 * a2
        for i in range(group):
            h = g * group + i
            n = own_n[j, h] * a1[i : i + 1] + xr_n[j, h].astype(jnp.float32) * a2[i : i + 1]
            if j == 0:
                own_n[0, h] = n
            else:
                zs_n[j, h] = n.astype(jnp.bfloat16)
        if j > 0:
            where = tok(2 * j)
            send(("nz", j, g), zs_n.at[j, heads_of(g)], zr_n.at[j, heads_of(g)], where)
            send(("sz", j, g), zs_s.at[j, g], zr_s.at[j, g], where)

    def attend_unit(j, g):
        def unit(r):
            h = g * group + r
            q = qbuf[2 * j * rows : (2 * j + 2) * rows, h * dim : (h + 1) * dim]
            return kbuf[h], vbuf[h], q, None

        def finish(r, n, m, l):
            h = g * group + r
            own_n[j, h] = n[:, :rows]
            own_s[j, g, r : r + 1, :] = m[:, :rows]
            own_s[j, g, group + r : group + r + 1, :] = l[:, :rows]
            xs_n[j, h] = n[:, rows:].astype(jnp.bfloat16)
            xs_s[j, g, r : r + 1, :] = m[:, rows:]
            xs_s[j, g, group + r : group + r + 1, :] = l[:, rows:]

        attend_units([functools.partial(unit, r) for r in range(group)], finish)
        send(("nx", j, g), xs_n.at[j, heads_of(g)], xr_n.at[j, heads_of(g)], tok(1))
        send(("sx", j, g), xs_s.at[j, g], xr_s.at[j, g], tok(1))

    def wait_queries(j):
        for k in (2 * j, 2 * j + 1):
            if k > 0:
                arrived(("qc", k), qpart(k, there), (sibling, ti))

    send_sibling(1)
    for j in range(pairs - 1, 0, -1):
        arrived(("qz", j), qnear(2 * j), tok(2 * j))
        send(("qx", j), qnear(2 * j), qnear(2 * j + 1), tok(1))
        send_across(2 * j)
    wait_queries(0)
    attend_unit(0, 0)
    for j in range(pairs - 1, 0, -1):
        arrived(("qx", j), qnear(2 * j + 1), tok(1))
        send_across(2 * j + 1)
        send_sibling(2 * j)
    attend_unit(0, 1)
    for j in range(pairs - 1, 0, -1):
        send_sibling(2 * j + 1)
    merge_x(0, 0)
    for k in range(n_tok - 1, 0, -1):
        cols = pl.ds(pl.multiple_of(peer[k] * dim, dim), dim)
        send(("oq", k), oq_ref.at[0, :, cols], oqbuf.at[pl.ds(k * qrows, qrows), :], tok(k))
    before = (0, 1)
    for j in range(pairs - 1, 0, -1):
        wait_queries(j)
        for g in range(2):
            attend_unit(j, g)
            merge_x(*before)
            before = (j, g)
    w_rows = w_ref.shape[0] // 2
    w_here = pl.ds(pl.multiple_of(mine * w_rows, w_rows), w_rows)
    w_there = pl.ds(pl.multiple_of((1 - mine) * w_rows, w_rows), w_rows)
    send(("wx",), w_ref.at[w_here, :], wbuf.at[w_here, :], tok(1))
    merge_x(*before)

    line = lax.div(ti, 2)
    middle = jnp.logical_and(line > 0, line < pairs - 1)

    def lat_part(slot, g):
        return lat.at[slot, pl.ds(g * group * dim, group * dim), :]

    def forward(slot, g):
        far, near = tok(2 * (pairs - 1)), tok(2)
        plan = {0: (3, far), 1: (2, far), 3: (2, near), 2: (3, near)}
        there_slot, where = plan[slot]
        return copy(
            ("lz", there_slot, g), lat_part(slot, g), lat_part(there_slot, g), where, ("fz", slot, g)
        )

    def pass_on(slot):
        for g in range(2):
            arrived(("lz", slot, g), lat_part(slot, g), tok(2))
            forward(slot, g).start()

    for g in range(2):
        for j in range(pairs - 1, 0, -1):
            arrived(("nz", j, g), zr_n.at[j, heads_of(g)], tok(2 * j))
            arrived(("sz", j, g), zr_s.at[j, g], tok(2 * j))
        peaks = [own_s[0, g, 0:group, :]] + [zr_s[j, g, 0:group, :] for j in range(1, pairs)]
        dens = [own_s[0, g, group:, :]] + [zr_s[j, g, group:, :] for j in range(1, pairs)]
        top = functools.reduce(jnp.maximum, peaks)
        scale = [jnp.exp2(p - top) for p in peaks]
        total = sum(d * s for d, s in zip(dens, scale))
        scale = [s / total for s in scale]
        for i in range(group):
            h = g * group + i
            n = own_n[0, h] * scale[0][i : i + 1]
            for j in range(1, pairs):
                n = n + zr_n[j, h].astype(jnp.float32) * scale[j][i : i + 1]
            lat[0, h * dim : (h + 1) * dim, :] = n.astype(jnp.bfloat16)
        send(("lz", 1, g), lat_part(0, g), lat_part(1, g), tok(2))

        @pl.when(middle)
        def _():
            forward(0, g).start()

    def mix_weights(source, place):
        for t in range(3):
            w_t = source[t * width : (t + 1) * width, :].T.astype(jnp.float32)
            gain = gain_ref[t * width : (t + 1) * width].reshape(1, width)
            at = 2 * t + place
            w3[at * dim : (at + 1) * dim, :] = (w_t * gain).astype(jnp.bfloat16)

    arrived(("wx",), wbuf.at[w_here, :], tok(1))
    send(("wc",), wbuf.at[w_here, :], wbuf.at[w_here, :], (sibling, ti))
    mix_weights(w_ref, 0)

    @pl.when(middle)
    def _():
        pass_on(1)

    arrived(("wc",), wbuf.at[w_there, :], (sibling, ti))
    mix_weights(wbuf, 1)

    def mix_rows(c):
        block = lat[c]
        wide = block.astype(jnp.float32)
        squares = jnp.sum(wide * wide, axis=0, keepdims=True)
        terms = jnp.dot(w3[...], block, preferred_element_type=jnp.float32)
        now[c] = terms[: 2 * dim]
        sq_own[c] = jnp.broadcast_to(squares, sq_own.shape[1:])
        sq = jnp.broadcast_to(squares, (16, rows)).astype(jnp.bfloat16)
        ts1[c, 0 : 2 * dim, :] = terms[2 * dim : 4 * dim].astype(jnp.bfloat16)
        ts1[c, 2 * dim :, :] = sq
        ts2[c, 0 : 2 * dim, :] = terms[4 * dim :].astype(jnp.bfloat16)
        ts2[c, 2 * dim :, :] = sq

        @pl.when(fi < n_frame - 1)
        def _():
            copy(("t1", c), ts1.at[c], tr1.at[c], (lax.rem(fi + 1, n_frame), ti)).start()

        @pl.when(fi < n_frame - 2)
        def _():
            copy(("t2", c), ts2.at[c], tr2.at[c], (lax.rem(fi + 2, n_frame), ti)).start()

    @pl.when(fi < 1)
    def _():
        tr1[...] = jnp.zeros_like(tr1)

    @pl.when(fi < 2)
    def _():
        tr2[...] = jnp.zeros_like(tr2)

    def finish_rows(c):
        @pl.when(fi >= 1)
        def _():
            copy(("t1", c), ts1.at[c], tr1.at[c], (lax.rem(fi + 1, n_frame), ti)).wait_recv()

        @pl.when(fi >= 2)
        def _():
            copy(("t2", c), ts2.at[c], tr2.at[c], (lax.rem(fi + 2, n_frame), ti)).wait_recv()

        before_one = tr1[c].astype(jnp.float32)
        before_two = tr2[c].astype(jnp.float32)
        summed = now[c] + before_one[: 2 * dim] + before_two[: 2 * dim]
        squares = sq_own[c, 0:1, :] + before_one[2 * dim : 2 * dim + 1] + before_two[2 * dim : 2 * dim + 1]
        z = summed * lax.rsqrt(squares / (3 * width) + 1e-06)
        mixed = (0.5 * z * (1.0 + lax.erf(z * math.sqrt(0.5)))).astype(jnp.bfloat16)
        msend[c] = mixed[dim:]
        send(("mx", c), msend.at[c], mixbuf.at[2 * c + 1], tok(1))
        mixbuf[2 * c] = mixed[:dim]

    @pl.when(middle)
    def _():
        pass_on(3)

    mix_rows(0)

    @pl.when(middle)
    def _():
        pass_on(2)

    @pl.when(jnp.logical_not(middle))
    def _():
        for g in range(2):
            arrived(("lz", 1, g), lat_part(1, g), tok(2))

    mix_rows(1)

    @pl.when(jnp.logical_not(middle))
    def _():
        for g in range(2):
            arrived(("lz", 2, g), lat_part(2, g), tok(2))

    finish_rows(0)
    mix_rows(2)

    @pl.when(jnp.logical_not(middle))
    def _():
        for g in range(2):
            arrived(("lz", 3, g), lat_part(3, g), tok(2))

    mix_rows(3)
    for c in range(1, pairs):
        finish_rows(c)
    for k in range(n_tok):
        if k % 2:
            arrived(("mx", k // 2), mixbuf.at[k], tok(1))
        block = mixbuf[k]
        mix_t[0:dim, k * rows : (k + 1) * rows] = block
        mix[k * rows : (k + 1) * rows, :] = block.T

    for k in range(1, n_tok):
        arrived(("oq", k), oqbuf.at[pl.ds(k * qrows, qrows), :], tok(k))
    mix_t[dim:, :] = jnp.ones((ONES, mix_t.shape[1]), jnp.bfloat16)

    def decode_unit(i):
        c = pairs - 1 - i
        return mix[...], mix_t[...], oqbuf[2 * c * qrows : (2 * c + 2) * qrows, :], factor

    def decode_finish(i, n, m, l):
        c = pairs - 1 - i
        o = (n / l).T
        for k in (2 * c, 2 * c + 1):
            part = o[(k - 2 * c) * qrows : (k - 2 * c + 1) * qrows]
            if k == 0:
                out_ref[0, :, own_cols] = part
            else:
                osend[k] = part.astype(jnp.bfloat16)
                send(("out", k), osend.at[k], obuf.at[k], tok(k))

    attend_units([functools.partial(decode_unit, i) for i in range(pairs)], decode_finish)
    for k in range(n_tok - 1, 0, -1):
        arrived(("out", k), obuf.at[k], tok(k))
        cols = pl.ds(pl.multiple_of(peer[k] * dim, dim), dim)
        out_ref[0, :, cols] = obuf[k].astype(jnp.float32)

    for c in started:
        c.wait_send()

    @pl.when(middle)
    def _():
        for g in range(2):
            for slot in range(pairs):
                forward(slot, g).wait_send()

    for c in range(pairs):

        @pl.when(fi < n_frame - 1)
        def _():
            copy(("t1", c), ts1.at[c], tr1.at[c], (lax.rem(fi + 1, n_frame), ti)).wait_send()

        @pl.when(fi < n_frame - 2)
        def _():
            copy(("t2", c), ts2.at[c], tr2.at[c], (lax.rem(fi + 2, n_frame), ti)).wait_send()


def local_fused(inputs, kv_weight, latent_queries, mix_gain, mix_weight, output_queries):
    n_tok = lax.axis_size("tok")
    n_frame = lax.axis_size("frame")
    pairs = n_tok // 2
    heads = HEADS
    dim = HEAD_DIM
    width = heads * dim
    n_in = inputs.shape[1]
    rows = latent_queries.shape[0]
    qrows = output_queries.shape[1]
    bf16, f32 = jnp.bfloat16, jnp.float32
    stats = (pairs, 2, heads, rows)
    block = (pairs, heads, dim, rows)
    n_ids = len(copy_ids(n_tok, pairs))
    vmem = pltpu.VMEM
    scratch = [
        vmem((n_tok * rows, width), bf16),
        vmem((heads, n_in, dim), bf16),
        vmem((heads, dim + ONES, n_in), bf16),
        vmem((3 * width, dim), bf16),
        vmem((6 * dim, width), bf16),
        vmem(block, f32), vmem(stats, f32),
        vmem(block, bf16), vmem(stats, f32),
        vmem(block, bf16), vmem(stats, f32),
        vmem(block, bf16), vmem(stats, f32),
        vmem(block, bf16), vmem(stats, f32),
        vmem((pairs, width, rows), bf16),
        vmem((pairs, 2 * dim, rows), f32),
        vmem((pairs, 8, rows), f32),
        vmem((pairs, 2 * dim + 16, rows), bf16),
        vmem((pairs, 2 * dim + 16, rows), bf16),
        vmem((pairs, 2 * dim + 16, rows), bf16),
        vmem((pairs, 2 * dim + 16, rows), bf16),
        vmem((pairs, dim, rows), bf16),
        vmem((n_tok, dim, rows), bf16),
        vmem((dim + ONES, n_tok * rows), bf16),
        vmem((n_tok * rows, dim), bf16),
        vmem((n_tok * qrows, dim), bf16),
        vmem((n_tok, qrows, dim), bf16),
        vmem((n_tok, qrows, dim), bf16),
        pltpu.SemaphoreType.DMA((n_ids,)),
        pltpu.SemaphoreType.DMA((n_ids,)),
    ]
    return pl.pallas_call(
        functools.partial(window_kernel, n_tok, n_frame),
        out_shape=jax.ShapeDtypeStruct((1, qrows, width), f32),
        in_specs=[pl.BlockSpec(memory_space=pltpu.VMEM)] * 6,
        out_specs=pl.BlockSpec(memory_space=pltpu.VMEM),
        scratch_shapes=scratch,
        compiler_params=pltpu.CompilerParams(
            collective_id=0, has_side_effects=True, vmem_limit_bytes=56 * 1024 * 1024
        ),
    )(inputs, kv_weight, latent_queries, mix_gain, mix_weight, output_queries)


def pick_local(mesh):
    n_tok, n_frame = mesh.shape["tok"], mesh.shape["frame"]
    fits = n_tok == HEADS and n_frame % 4 == 0
    return local_fused if fits else local


def solution(mesh):
    return jax.shard_map(
        pick_local(mesh),
        mesh=mesh,
        in_specs=(
            P("frame", "tok", None),
            P(),
            P("tok", None),
            P(),
            P(None, "tok"),
            P("frame", "tok", None),
        ),
        out_specs=P("frame", "tok", None),
        check_vma=False,
    )
```

```python
import functools
import math

import jax
import jax.numpy as jnp
from jax import lax
from jax.experimental import pallas as pl
from jax.experimental.pallas import tpu as pltpu
from jax.sharding import PartitionSpec as P

HEADS = 8
HEAD_DIM = 128


def from_behind(block, axis, distance):
    devices = range(lax.axis_size(axis))
    route = [(i - distance, i) for i in devices if i - distance in devices]
    return lax.ppermute(block, axis, route)


def attend_heads(queries, keys, values, head_count, head_dim):
    maxima = []
    numers = []
    denoms = []
    for head_index in range(head_count):
        low_col = head_index * head_dim
        high_col = low_col + head_dim
        scores = lax.dot_general(
            queries[:, low_col:high_col],
            keys[:, low_col:high_col],
            (((1,), (1,)), ((), ())),
            preferred_element_type=jnp.float32,
        ) / math.sqrt(head_dim)
        row_peak = jnp.max(scores, axis=1)
        weights = jnp.exp(scores - row_peak[:, None])
        denoms.append(jnp.sum(weights, axis=1))
        numers.append(
            jnp.dot(
                weights.astype(jnp.bfloat16),
                values[:, low_col:high_col],
                preferred_element_type=jnp.float32,
            )
        )
        maxima.append(row_peak)
    return (jnp.stack(maxima, axis=1), jnp.concatenate(numers, axis=1), jnp.stack(denoms, axis=1))


def finish_latents(numerator, denominator, head_count, head_dim):
    row_count = numerator.shape[0]
    shaped = numerator.reshape(row_count, head_count, head_dim) / denominator[:, :, None]
    return shaped.reshape(row_count, head_count * head_dim).astype(jnp.bfloat16)


def project_cols(latent_part, gain_part, weight_part):
    scaled = (latent_part.astype(jnp.float32) * gain_part).astype(jnp.bfloat16)
    return lax.dot_general(
        weight_part, scaled, (((0,), (1,)), ((), ())), preferred_element_type=jnp.float32
    )


def local(inputs, kv_weight, latent_queries, mix_gain, mix_weight, output_queries):
    head_count = HEADS
    head_dim = HEAD_DIM
    latent_width = head_count * head_dim
    frame_inputs = inputs[0]
    queries = lax.all_gather(latent_queries, "tok", axis=0, tiled=True)
    key_values = jnp.dot(frame_inputs, kv_weight, preferred_element_type=jnp.float32).astype(
        jnp.bfloat16
    )
    maxima, numers, denoms = attend_heads(
        queries, key_values[:, :latent_width], key_values[:, latent_width:], head_count, head_dim
    )
    peak_all = lax.pmax(maxima.astype(jnp.bfloat16), "tok").astype(maxima.dtype)
    rescale = jnp.exp(maxima - peak_all)
    latent_count = queries.shape[0]
    numer_terms = (
        numers.reshape(latent_count, head_count, head_dim) * rescale[:, :, None]
    ).reshape(latent_count, latent_width)
    denom_terms = denoms * rescale
    numerator, denominator = (
        lax.psum(numer_terms.astype(jnp.bfloat16), "tok").astype(jnp.float32),
        lax.psum(denom_terms.astype(jnp.bfloat16), "tok").astype(jnp.float32),
    )
    latents = finish_latents(numerator, denominator, head_count, head_dim)
    latent_f32 = latents.astype(jnp.float32)
    own_squares = jnp.sum(latent_f32 * latent_f32, axis=1)
    term_now = project_cols(latents, mix_gain[:latent_width], mix_weight[:latent_width])
    term_one, squares_one = (
        from_behind(
            project_cols(
                latents,
                mix_gain[latent_width : 2 * latent_width],
                mix_weight[latent_width : 2 * latent_width],
            ).astype(jnp.bfloat16),
            "frame",
            1,
        ).astype(jnp.float32),
        from_behind(own_squares.astype(jnp.bfloat16), "frame", 1).astype(own_squares.dtype),
    )
    term_two, squares_two = (
        from_behind(
            project_cols(
                latents, mix_gain[2 * latent_width :], mix_weight[2 * latent_width :]
            ).astype(jnp.bfloat16),
            "frame",
            2,
        ).astype(jnp.float32),
        from_behind(own_squares.astype(jnp.bfloat16), "frame", 2).astype(own_squares.dtype),
    )
    summed = term_now + term_one + term_two
    squares = own_squares + squares_one + squares_two
    inverse = lax.rsqrt(squares / (3 * latent_width) + 1e-06)
    mixed_cols = jax.nn.gelu(summed * inverse[None, :], approximate=False).astype(jnp.bfloat16)
    mixed_t = lax.all_gather(mixed_cols, "tok", axis=0, tiled=True)
    frame_queries = output_queries[0]
    pieces = []
    for head_index in range(head_count):
        low_col = head_index * head_dim
        high_col = low_col + head_dim
        scores = jnp.dot(
            frame_queries[:, low_col:high_col],
            mixed_t[low_col:high_col],
            preferred_element_type=jnp.float32,
        ) / math.sqrt(head_dim)
        row_peak = jnp.max(scores, axis=1)
        weights = jnp.exp(scores - row_peak[:, None])
        denom_sum = jnp.sum(weights, axis=1)
        head_sum = lax.dot_general(
            weights.astype(jnp.bfloat16),
            mixed_t[low_col:high_col],
            (((1,), (1,)), ((), ())),
            preferred_element_type=jnp.float32,
        )
        pieces.append(head_sum / denom_sum[:, None])
    result = jnp.concatenate(pieces, axis=1)
    return result[None]


MESH = pl.DeviceIdType.MESH
LOG2E = 1.4426950408889634
ONES = 16


def dot_nt(a, b):
    return lax.dot_general(a, b, (((1,), (1,)), ((), ())), preferred_element_type=jnp.float32)


def attend_units(units, finish):
    def score(unit):
        keys, _, queries, factor = unit()
        scores = dot_nt(keys, queries)
        return scores if factor is None else scores * factor

    ahead = score(units[0])
    for i, unit in enumerate(units):
        scores = ahead
        if i + 1 < len(units):
            ahead = score(units[i + 1])
        peak = jnp.max(scores, axis=0, keepdims=True)
        weights = jnp.exp2(scores - peak).astype(jnp.bfloat16)
        values = unit()[1]
        numer = jnp.dot(values, weights, preferred_element_type=jnp.float32)
        dim = values.shape[0] - ONES
        finish(i, numer[:dim], peak, numer[dim : dim + 1])


def copy_ids(n_tok, pairs):
    names = []
    for j in range(1, pairs):
        names += [("qz", j), ("qx", j)]
    for j in range(pairs):
        names += [("t1", j), ("t2", j), ("mx", j)]
        for g in range(2):
            names += [(n, j, g) for n in ("nx", "sx", "nz", "sz", "lz", "fz")]
    for k in range(1, n_tok):
        names += [("qc", k), ("qy", k), ("oq", k), ("out", k)]
    names += [("qx", 0), ("wx",), ("wc",)]
    return {name: i for i, name in enumerate(names)}


def window_kernel(
    n_tok, n_frame, x_ref, kvw_ref, lq_ref, gain_ref, w_ref, oq_ref, out_ref,
    qbuf, kbuf, vbuf, wbuf, w3, own_n, own_s, xs_n, xs_s, xr_n, xr_s, zs_n, zs_s, zr_n, zr_s,
    lat, now, sq_own, ts1, ts2, tr1, tr2, msend, mixbuf, mix_t, mix, oqbuf, dec_n, dec_s, osend, obuf, send_sem, recv_sem,
):
    heads = n_tok
    pairs = n_tok // 2
    rows = lq_ref.shape[0]
    dim = w_ref.shape[1]
    width = heads * dim
    qrows = oq_ref.shape[1]
    factor = LOG2E / math.sqrt(dim)
    ids = copy_ids(n_tok, pairs)
    fi = lax.axis_index("frame")
    ti = lax.axis_index("tok")
    half = rows // 2
    mine = lax.rem(fi, 2)
    sibling = fi + 1 - 2 * mine
    started = []

    def flip(k):
        out = 0
        bit = 1
        while bit < n_tok:
            b = lax.rem(lax.div(ti, bit), 2)
            out = out + bit * ((1 - b) if (k & bit) else b)
            bit *= 2
        return out

    peer = [flip(k) for k in range(n_tok)]

    def copy(name, src, dst, where, send_name=None):
        return pltpu.make_async_remote_copy(
            src_ref=src, dst_ref=dst,
            send_sem=send_sem.at[ids[send_name or name]], recv_sem=recv_sem.at[ids[name]],
            device_id=where, device_id_type=MESH,
        )

    def send(name, src, dst, where):
        c = copy(name, src, dst, where)
        c.start()
        started.append(c)

    def arrived(name, dst, where):
        copy(name, dst, dst, where).wait_recv()

    def tok(k):
        return (fi, peer[k])

    barrier = pltpu.get_barrier_semaphore()
    for k in range(1, n_tok):
        pl.semaphore_signal(barrier, inc=1, device_id=tok(k), device_id_type=MESH)
    for o in range(1, n_frame):
        pl.semaphore_signal(
            barrier, inc=1, device_id=(lax.rem(fi + o, n_frame), ti), device_id_type=MESH
        )
    pl.semaphore_wait(barrier, n_tok - 1 + n_frame - 1)

    here = pl.multiple_of(mine * half, half)
    there = pl.multiple_of((1 - mine) * half, half)

    quarter = half // 2
    plane = lax.rem(lax.div(fi, 2), 2)
    across = fi + 2 - 4 * plane
    near_rows = pl.multiple_of(here + plane * quarter, quarter)
    far_rows = pl.multiple_of(here + (1 - plane) * quarter, quarter)

    def qpart(k, off, count=half):
        return qbuf.at[pl.ds(k * rows + off, count), :]

    def qnear(k):
        return qpart(k, near_rows, quarter)

    def send_across(k):
        send(("qy", k), qnear(k), qnear(k), (across, ti))

    def send_sibling(k):
        arrived(("qy", k), qpart(k, far_rows, quarter), (across, ti))
        send(("qc", k), qpart(k, here), qpart(k, here), (sibling, ti))

    own_part = lq_ref.at[pl.ds(near_rows, quarter), :]
    for j in range(pairs - 1, 0, -1):
        send(("qz", j), own_part, qnear(2 * j), tok(2 * j))
    send(("qx", 0), own_part, qnear(1), tok(1))
    qbuf[0:rows, :] = lq_ref[...]
    own_cols = pl.ds(pl.multiple_of(ti * dim, dim), dim)
    oqbuf[0:qrows, :] = oq_ref[0, :, own_cols]

    def project_keys(i, carry):
        cols = pl.ds(pl.multiple_of(i * 2 * dim, 2 * dim), 2 * dim)
        k = jnp.dot(x_ref[0], kvw_ref[:, cols], preferred_element_type=jnp.float32)
        k = (k * factor).astype(jnp.bfloat16)
        kbuf[2 * i] = k[:, :dim]
        kbuf[2 * i + 1] = k[:, dim:]
        return carry

    lax.fori_loop(0, heads // 2, project_keys, 0, unroll=True)

    arrived(("qx", 0), qnear(1), tok(1))
    send_across(1)
    def project_values(i, carry):
        cols = pl.ds(pl.multiple_of(width + i * 2 * dim, 2 * dim), 2 * dim)
        v = jnp.dot(x_ref[0], kvw_ref[:, cols], preferred_element_type=jnp.float32)
        v = v.astype(jnp.bfloat16).T
        vbuf[2 * i, 0:dim, :] = v[:dim]
        vbuf[2 * i + 1, 0:dim, :] = v[dim:]
        return carry

    vbuf[:, dim:, :] = jnp.ones((heads, ONES, vbuf.shape[2]), jnp.bfloat16)
    lax.fori_loop(0, heads // 2, project_values, 0, unroll=True)

    group = heads // 2

    def heads_of(g):
        return pl.ds(g * group, group)

    def merge_x(j, g):
        arrived(("nx", j, g), xr_n.at[j, heads_of(g)], tok(1))
        arrived(("sx", j, g), xr_s.at[j, g], tok(1))
        m1, l1 = own_s[j, g, 0:group, :], own_s[j, g, group:, :]
        m2, l2 = xr_s[j, g, 0:group, :], xr_s[j, g, group:, :]
        m = jnp.maximum(m1, m2)
        a1, a2 = jnp.exp2(m1 - m), jnp.exp2(m2 - m)
        target = own_s if j == 0 else zs_s
        target[j, g, 0:group, :] = m
        target[j, g, group:, :] = l1 * a1 + l2 * a2
        for i in range(group):
            h = g * group + i
            n = own_n[j, h] * a1[i : i + 1] + xr_n[j, h].astype(jnp.float32) * a2[i : i + 1]
            if j == 0:
                own_n[0, h] = n
            else:
                zs_n[j, h] = n.astype(jnp.bfloat16)
        if j > 0:
            where = tok(2 * j)
            send(("nz", j, g), zs_n.at[j, heads_of(g)], zr_n.at[j, heads_of(g)], where)
            send(("sz", j, g), zs_s.at[j, g], zr_s.at[j, g], where)

    def attend_unit(j, g):
        def unit(r):
            h = g * group + r
            q = qbuf[2 * j * rows : (2 * j + 2) * rows, h * dim : (h + 1) * dim]
            return kbuf[h], vbuf[h], q, None

        def finish(r, n, m, l):
            h = g * group + r
            own_n[j, h] = n[:, :rows]
            own_s[j, g, r : r + 1, :] = m[:, :rows]
            own_s[j, g, group + r : group + r + 1, :] = l[:, :rows]
            xs_n[j, h] = n[:, rows:].astype(jnp.bfloat16)
            xs_s[j, g, r : r + 1, :] = m[:, rows:]
            xs_s[j, g, group + r : group + r + 1, :] = l[:, rows:]

        attend_units([functools.partial(unit, r) for r in range(group)], finish)
        send(("nx", j, g), xs_n.at[j, heads_of(g)], xr_n.at[j, heads_of(g)], tok(1))
        send(("sx", j, g), xs_s.at[j, g], xr_s.at[j, g], tok(1))

    def wait_queries(j):
        for k in (2 * j, 2 * j + 1):
            if k > 0:
                arrived(("qc", k), qpart(k, there), (sibling, ti))

    send_sibling(1)
    for j in range(pairs - 1, 0, -1):
        arrived(("qz", j), qnear(2 * j), tok(2 * j))
        send(("qx", j), qnear(2 * j), qnear(2 * j + 1), tok(1))
        send_across(2 * j)
    wait_queries(0)
    attend_unit(0, 0)
    for j in range(pairs - 1, 0, -1):
        arrived(("qx", j), qnear(2 * j + 1), tok(1))
        send_across(2 * j + 1)
        send_sibling(2 * j)
    attend_unit(0, 1)
    for j in range(pairs - 1, 0, -1):
        send_sibling(2 * j + 1)
    merge_x(0, 0)
    for k in range(n_tok - 1, 0, -1):
        cols = pl.ds(pl.multiple_of(peer[k] * dim, dim), dim)
        send(("oq", k), oq_ref.at[0, :, cols], oqbuf.at[pl.ds(k * qrows, qrows), :], tok(k))
    before = (0, 1)
    for j in range(pairs - 1, 0, -1):
        wait_queries(j)
        for g in range(2):
            attend_unit(j, g)
            merge_x(*before)
            before = (j, g)
    w_rows = w_ref.shape[0] // 2
    w_here = pl.ds(pl.multiple_of(mine * w_rows, w_rows), w_rows)
    w_there = pl.ds(pl.multiple_of((1 - mine) * w_rows, w_rows), w_rows)
    send(("wx",), w_ref.at[w_here, :], wbuf.at[w_here, :], tok(1))
    merge_x(*before)

    line = lax.div(ti, 2)
    middle = jnp.logical_and(line > 0, line < pairs - 1)

    def lat_part(slot, g):
        return lat.at[slot, pl.ds(g * group * dim, group * dim), :]

    def forward(slot, g):
        far, near = tok(2 * (pairs - 1)), tok(2)
        plan = {0: (3, far), 1: (2, far), 3: (2, near), 2: (3, near)}
        there_slot, where = plan[slot]
        return copy(
            ("lz", there_slot, g), lat_part(slot, g), lat_part(there_slot, g), where, ("fz", slot, g)
        )

    def pass_on(slot):
        for g in range(2):
            arrived(("lz", slot, g), lat_part(slot, g), tok(2))
            forward(slot, g).start()

    def mix_weights(source, place):
        for t in range(3):
            w_t = source[t * width : (t + 1) * width, :].T.astype(jnp.float32)
            gain = gain_ref[t * width : (t + 1) * width].reshape(1, width)
            at = 2 * t + place
            w3[at * dim : (at + 1) * dim, :] = (w_t * gain).astype(jnp.bfloat16)

    mix_weights(w_ref, 0)

    for g in range(2):
        for j in range(pairs - 1, 0, -1):
            arrived(("nz", j, g), zr_n.at[j, heads_of(g)], tok(2 * j))
            arrived(("sz", j, g), zr_s.at[j, g], tok(2 * j))
        peaks = [own_s[0, g, 0:group, :]] + [zr_s[j, g, 0:group, :] for j in range(1, pairs)]
        dens = [own_s[0, g, group:, :]] + [zr_s[j, g, group:, :] for j in range(1, pairs)]
        top = functools.reduce(jnp.maximum, peaks)
        scale = [jnp.exp2(p - top) for p in peaks]
        total = sum(d * s for d, s in zip(dens, scale))
        scale = [s / total for s in scale]
        for i in range(group):
            h = g * group + i
            n = own_n[0, h] * scale[0][i : i + 1]
            for j in range(1, pairs):
                n = n + zr_n[j, h].astype(jnp.float32) * scale[j][i : i + 1]
            lat[0, h * dim : (h + 1) * dim, :] = n.astype(jnp.bfloat16)
        send(("lz", 1, g), lat_part(0, g), lat_part(1, g), tok(2))

        @pl.when(middle)
        def _():
            forward(0, g).start()

    arrived(("wx",), wbuf.at[w_here, :], tok(1))
    send(("wc",), wbuf.at[w_here, :], wbuf.at[w_here, :], (sibling, ti))

    @pl.when(middle)
    def _():
        pass_on(1)

    arrived(("wc",), wbuf.at[w_there, :], (sibling, ti))
    mix_weights(wbuf, 1)

    def mix_rows(c):
        block = lat[c]
        wide = block.astype(jnp.float32)
        squares = jnp.sum(wide * wide, axis=0, keepdims=True)
        terms = jnp.dot(w3[...], block, preferred_element_type=jnp.float32)
        now[c] = terms[: 2 * dim]
        sq_own[c] = jnp.broadcast_to(squares, sq_own.shape[1:])
        sq = jnp.broadcast_to(squares, (16, rows)).astype(jnp.bfloat16)
        ts1[c, 0 : 2 * dim, :] = terms[2 * dim : 4 * dim].astype(jnp.bfloat16)
        ts1[c, 2 * dim :, :] = sq
        ts2[c, 0 : 2 * dim, :] = terms[4 * dim :].astype(jnp.bfloat16)
        ts2[c, 2 * dim :, :] = sq

        @pl.when(fi < n_frame - 1)
        def _():
            copy(("t1", c), ts1.at[c], tr1.at[c], (lax.rem(fi + 1, n_frame), ti)).start()

        @pl.when(fi < n_frame - 2)
        def _():
            copy(("t2", c), ts2.at[c], tr2.at[c], (lax.rem(fi + 2, n_frame), ti)).start()

    @pl.when(fi < 1)
    def _():
        tr1[...] = jnp.zeros_like(tr1)

    @pl.when(fi < 2)
    def _():
        tr2[...] = jnp.zeros_like(tr2)

    def finish_rows(c):
        @pl.when(fi >= 1)
        def _():
            copy(("t1", c), ts1.at[c], tr1.at[c], (lax.rem(fi + 1, n_frame), ti)).wait_recv()

        @pl.when(fi >= 2)
        def _():
            copy(("t2", c), ts2.at[c], tr2.at[c], (lax.rem(fi + 2, n_frame), ti)).wait_recv()

        before_one = tr1[c].astype(jnp.float32)
        before_two = tr2[c].astype(jnp.float32)
        summed = now[c] + before_one[: 2 * dim] + before_two[: 2 * dim]
        squares = sq_own[c, 0:1, :] + before_one[2 * dim : 2 * dim + 1] + before_two[2 * dim : 2 * dim + 1]
        z = summed * lax.rsqrt(squares / (3 * width) + 1e-06)
        mixed = (0.5 * z * (1.0 + lax.erf(z * math.sqrt(0.5)))).astype(jnp.bfloat16)
        msend[c] = mixed[dim:]
        send(("mx", c), msend.at[c], mixbuf.at[2 * c + 1], tok(1))
        mixbuf[2 * c] = mixed[:dim]

    mix_t[dim:, :] = jnp.ones((ONES, mix_t.shape[1]), jnp.bfloat16)

    def decode_half(part):
        span = n_tok // 2
        for k in range(part * span, (part + 1) * span):
            if k % 2:
                arrived(("mx", k // 2), mixbuf.at[k], tok(1))
            block = mixbuf[k]
            mix_t[0:dim, k * rows : (k + 1) * rows] = block
            mix[k * rows : (k + 1) * rows, :] = block.T
        low, high = part * span * rows, (part + 1) * span * rows

        def unit(i):
            c = pairs - 1 - i
            q = oqbuf[2 * c * qrows : (2 * c + 2) * qrows, :]
            return mix[low:high, :], mix_t[:, low:high], q, factor

        def keep(i, n, m, l):
            dec_n[i] = n
            dec_s[i, 0:1, :] = m
            dec_s[i, 8:9, :] = l

        def finish(i, n, m, l):
            c = pairs - 1 - i
            m0 = dec_s[i, 0:1, :]
            top = jnp.maximum(m, m0)
            a, a0 = jnp.exp2(m - top), jnp.exp2(m0 - top)
            den = l * a + dec_s[i, 8:9, :] * a0
            o = (n * (a / den) + dec_n[i] * (a0 / den)).T
            for k in (2 * c, 2 * c + 1):
                rows_k = o[(k - 2 * c) * qrows : (k - 2 * c + 1) * qrows]
                if k == 0:
                    out_ref[0, :, own_cols] = rows_k
                else:
                    osend[k] = rows_k.astype(jnp.bfloat16)
                    send(("out", k), osend.at[k], obuf.at[k], tok(k))

        units = [functools.partial(unit, i) for i in range(pairs)]
        attend_units(units, finish if part else keep)

    for k in range(1, n_tok):
        arrived(("oq", k), oqbuf.at[pl.ds(k * qrows, qrows), :], tok(k))

    @pl.when(middle)
    def _():
        pass_on(3)

    mix_rows(0)

    @pl.when(middle)
    def _():
        pass_on(2)

    @pl.when(jnp.logical_not(middle))
    def _():
        for g in range(2):
            arrived(("lz", 1, g), lat_part(1, g), tok(2))

    mix_rows(1)

    @pl.when(jnp.logical_not(middle))
    def _():
        for g in range(2):
            arrived(("lz", 2, g), lat_part(2, g), tok(2))

    finish_rows(0)
    mix_rows(2)
    finish_rows(1)
    decode_half(0)

    @pl.when(jnp.logical_not(middle))
    def _():
        for g in range(2):
            arrived(("lz", 3, g), lat_part(3, g), tok(2))

    mix_rows(3)
    for c in range(pairs // 2, pairs):
        finish_rows(c)
    decode_half(1)

    for k in range(n_tok - 1, 0, -1):
        arrived(("out", k), obuf.at[k], tok(k))
        cols = pl.ds(pl.multiple_of(peer[k] * dim, dim), dim)
        out_ref[0, :, cols] = obuf[k].astype(jnp.float32)

    for c in started:
        c.wait_send()

    @pl.when(middle)
    def _():
        for g in range(2):
            for slot in range(pairs):
                forward(slot, g).wait_send()

    for c in range(pairs):

        @pl.when(fi < n_frame - 1)
        def _():
            copy(("t1", c), ts1.at[c], tr1.at[c], (lax.rem(fi + 1, n_frame), ti)).wait_send()

        @pl.when(fi < n_frame - 2)
        def _():
            copy(("t2", c), ts2.at[c], tr2.at[c], (lax.rem(fi + 2, n_frame), ti)).wait_send()


def local_fused(inputs, kv_weight, latent_queries, mix_gain, mix_weight, output_queries):
    n_tok = lax.axis_size("tok")
    n_frame = lax.axis_size("frame")
    pairs = n_tok // 2
    heads = HEADS
    dim = HEAD_DIM
    width = heads * dim
    n_in = inputs.shape[1]
    rows = latent_queries.shape[0]
    qrows = output_queries.shape[1]
    bf16, f32 = jnp.bfloat16, jnp.float32
    stats = (pairs, 2, heads, rows)
    block = (pairs, heads, dim, rows)
    n_ids = len(copy_ids(n_tok, pairs))
    vmem = pltpu.VMEM
    scratch = [
        vmem((n_tok * rows, width), bf16),
        vmem((heads, n_in, dim), bf16),
        vmem((heads, dim + ONES, n_in), bf16),
        vmem((3 * width, dim), bf16),
        vmem((6 * dim, width), bf16),
        vmem(block, f32), vmem(stats, f32),
        vmem(block, bf16), vmem(stats, f32),
        vmem(block, bf16), vmem(stats, f32),
        vmem(block, bf16), vmem(stats, f32),
        vmem(block, bf16), vmem(stats, f32),
        vmem((pairs, width, rows), bf16),
        vmem((pairs, 2 * dim, rows), f32),
        vmem((pairs, 8, rows), f32),
        vmem((pairs, 2 * dim + 16, rows), bf16),
        vmem((pairs, 2 * dim + 16, rows), bf16),
        vmem((pairs, 2 * dim + 16, rows), bf16),
        vmem((pairs, 2 * dim + 16, rows), bf16),
        vmem((pairs, dim, rows), bf16),
        vmem((n_tok, dim, rows), bf16),
        vmem((dim + ONES, n_tok * rows), bf16),
        vmem((n_tok * rows, dim), bf16),
        vmem((n_tok * qrows, dim), bf16),
        vmem((pairs, dim, 2 * qrows), f32), vmem((pairs, 16, 2 * qrows), f32),
        vmem((n_tok, qrows, dim), bf16),
        vmem((n_tok, qrows, dim), bf16),
        pltpu.SemaphoreType.DMA((n_ids,)),
        pltpu.SemaphoreType.DMA((n_ids,)),
    ]
    return pl.pallas_call(
        functools.partial(window_kernel, n_tok, n_frame),
        out_shape=jax.ShapeDtypeStruct((1, qrows, width), f32),
        in_specs=[pl.BlockSpec(memory_space=pltpu.VMEM)] * 6,
        out_specs=pl.BlockSpec(memory_space=pltpu.VMEM),
        scratch_shapes=scratch,
        compiler_params=pltpu.CompilerParams(
            collective_id=0, has_side_effects=True, vmem_limit_bytes=56 * 1024 * 1024
        ),
    )(inputs, kv_weight, latent_queries, mix_gain, mix_weight, output_queries)


def pick_local(mesh):
    n_tok, n_frame = mesh.shape["tok"], mesh.shape["frame"]
    fits = n_tok == HEADS and n_frame % 4 == 0
    return local_fused if fits else local


def solution(mesh):
    return jax.shard_map(
        pick_local(mesh),
        mesh=mesh,
        in_specs=(
            P("frame", "tok", None),
            P(),
            P("tok", None),
            P(),
            P(None, "tok"),
            P("frame", "tok", None),
        ),
        out_specs=P("frame", "tok", None),
        check_vma=False,
    )
```
